256 devices in a mesh: expert: 64 (over x, z, core), chan: 4 (over y).
Axes of the slice: x: 4, y: 4, z: 8, core: 2. Of those that a mesh axis runs over, the one named last changes fastest.
Arguments:
- rows_in: bfloat16 [2048, 6144], P('expert', 'chan'), may hold values from -6 to 6
- expert_picks: int32 [2048, 2], P('expert'), may hold values from 0 to 3, all different within a row; in each aligned block of 32 rows (0 to 31, 32 to 63, ...) at most 18 rows name the same one
- latent_ids: int32 [2048, 2, 32], P('expert'), may hold values from 0 to 8191, as said below
- enc_weight: bfloat16 [6144, 32768], P('chan', 'expert'), may hold values from -0.078125 to 0.078125
- dec_weight: bfloat16 [32768, 6144], P('expert', 'chan'), may hold values from -0.375 to 0.375
Outputs:
- recon_error: bfloat16 [2048, 6144], P('expert', 'chan')
- enc_grad: float32 [6144, 32768], P('chan', 'expert')
- dec_grad: float32 [32768, 6144], P('expert', 'chan')
The draws below stay inside these ranges and needn't reach their ends.
Inputs may be any that keep to these rules, and one draw needn't show every extreme that they name: `expert_picks`: A row's two experts differ; among the 32 rows of one device at most 18 name one expert. latent_ids[r, j, k] lies in k * 256 to (k + 1) * 256 - 1 and numbers a latent of expert expert_picks[r, j].
All inputs are finite; a program needn't handle non-finite values.
Results may differ from the reference program's by a relative error of at most 0.0095.
Values may be sent and summed in bfloat16 or wider, within the bound.
A program may use at most 128 MiB of HBM per device.

```python
import math
import jax
import jax.numpy as jnp
import numpy as np

C = 6144
LAT = 8192
EXPERTS = 4
TOPK = 32
ROW_DEV = 32
CAP = 18
ROWS = 2048
LAT_ALL = 32768


def draw_latent_ids(key, part):
    stride = LAT // TOPK
    offsets = jax.random.randint(key, (ROWS, 2, TOPK), 0, stride, dtype=jnp.int32)
    starts = jnp.arange(TOPK, dtype=jnp.int32) * stride
    return offsets + starts[None, None, :]


def shard_levels(stream_key, extent, split, low, top_value):
    gain, own = 1.0, jax.random.fold_in(stream_key, 6)
    for dim, parts in split:
        steps = jnp.exp(jax.random.uniform(jax.random.fold_in(own, dim), (parts,), jnp.float32, low / len(split), top_value / len(split)))
        gain = gain * jnp.repeat(steps, extent[dim] // parts).reshape([-1 if axis == dim else 1 for axis in range(len(extent))])
    return gain


def assign_block(own_key, own, number, rows, amount, top, most, slope):
    order = jax.random.permutation(own_key, amount)
    heavy_load, ordinary = portions_of(amount, rows * top, most, slope, True), portions_of(amount, rows * top, most, slope, False)
    places = jnp.arange(amount)

    def named(sizes, offset_by):
        used = int((sizes > 0).sum())
        fixed = max(1, used // 4)
        moved = fixed + (places - fixed + offset_by * (used - fixed)) % max(1, amount - fixed)
        return jnp.zeros((amount,), jnp.int32).at[order[jnp.where(places < fixed, places, moved)]].set(jnp.asarray(sizes, jnp.int32))

    sizes = jnp.where(number % 4 == 0, named(heavy_load, number // 4), named(ordinary, number - number // 4 - 1))
    mixed = jax.random.permutation(jax.random.fold_in(own, 3), amount)
    giver, receiver = mixed[0:amount // 2 * 2:2], mixed[1:amount // 2 * 2:2]
    slack = jnp.minimum(sizes[giver] - 1, most - sizes[receiver]) // 2
    slack = jnp.where((giver == order[0]) | (receiver == order[0]) | (sizes[receiver] == 0), 0, jnp.maximum(slack, 0))
    moved = jax.random.randint(jax.random.fold_in(own, 4), (amount // 2,), 0, 1 << 20) % (slack + 1)
    sizes = sizes.at[giver].add(-moved).at[receiver].add(moved)
    labels = jnp.searchsorted(jnp.cumsum(sizes), jnp.arange(rows * top), side="right").astype(jnp.int32)
    table = labels.reshape(top, rows).T
    table = table[jax.random.permutation(jax.random.fold_in(own, 1), rows)]
    offset_by = jax.random.randint(jax.random.fold_in(own, 2), (rows, 1), 0, top)
    return jnp.take_along_axis(table, (jnp.arange(top)[None, :] + offset_by) % top, axis=1)


def portions_of(number_of, total, limit, lean, full):
    weights = [(1 << 20) // math.isqrt(rank ** lean) + 1 for rank in range(1, number_of + 1)]
    largest = limit if full else min(limit, max(-(-total // number_of), total * weights[0] // sum(weights)))
    least = 1 if total - largest >= number_of - 1 else 0
    given, rest = [largest] + [least] * (number_of - 1), total - largest - least * (number_of - 1)
    while rest > 0:
        candidates = [i for i in range(1, number_of) if given[i] < largest] or [i for i in range(1, number_of) if given[i] < limit]
        mass, left = sum([weights[i] for i in candidates]), rest
        for i in candidates:
            addition = min(limit - given[i], max(1, left * weights[i] // mass), rest)
            given[i] = given[i] + addition
            rest = rest - addition
    return np.array(given)


def centred(stream_key, extent, deviation, reach, split=(), kind=jnp.bfloat16):
    gain = shard_levels(stream_key, extent, split, -0.22, 0.18) if split else 1.0
    result = jax.random.normal(stream_key, extent, jnp.float32) * deviation * gain
    return jnp.minimum(jnp.maximum(result, -reach), reach).astype(kind)


def setup_inputs(seed: int = 0) -> dict:
    key_list = jax.random.split(jax.random.key(seed), 6)
    rows_in = centred(key_list[0], (ROWS, C), 1.0, 6.0, ((0, 64), (1, 4)))
    expert_picks_keys = jax.random.split(jax.random.fold_in(key_list[1], 1), ROWS // ROW_DEV)
    expert_picks_turns = jax.random.permutation(jax.random.fold_in(key_list[1], 3), ROWS // ROW_DEV)
    expert_picks = jax.vmap(lambda own, number: assign_block(jax.random.fold_in(key_list[1], 2), own, number, ROW_DEV, EXPERTS, 2, CAP, 2))(expert_picks_keys, expert_picks_turns).reshape((ROWS, 2))
    latent_ids = draw_latent_ids(jax.random.fold_in(key_list[5], 71), 0)
    enc_weight = centred(key_list[3], (C, LAT_ALL), C ** -0.5, 0.078125, ((0, 4), (1, 64)))
    dec_weight = centred(key_list[4], (LAT_ALL, C), (8 * TOPK) ** -0.5, 0.375, ((0, 64), (1, 4)))
    return dict(rows_in=rows_in, expert_picks=expert_picks, latent_ids=latent_ids, enc_weight=enc_weight, dec_weight=dec_weight)


def expert_parts(rows_in, expert_picks, latent_ids, enc_weight, dec_weight, expert_id):
    stride = LAT // TOPK
    hit_table = (expert_picks == expert_id).astype(jnp.int32)
    chosen = jnp.sum(hit_table[:, :, None] * (latent_ids + 1), axis=1) - 1
    spread = jnp.repeat(chosen, stride, axis=1)
    live_mask = spread == jnp.arange(LAT, dtype=jnp.int32)[None, :]
    enc_part = enc_weight[:, expert_id * LAT:(expert_id + 1) * LAT]
    dec_part = dec_weight[expert_id * LAT:(expert_id + 1) * LAT, :]
    preact = jnp.dot(rows_in, enc_part, preferred_element_type=jnp.float32)
    activation = jnp.where(live_mask, preact, jnp.float32(0.0)).astype(jnp.bfloat16)
    return live_mask, activation, dec_part


def reference(rows_in, expert_picks, latent_ids, enc_weight, dec_weight):
    recon = jnp.zeros((rows_in.shape[0], rows_in.shape[1]), jnp.float32)
    for expert_id in range(EXPERTS):
        live_mask, activation, dec_part = expert_parts(rows_in, expert_picks, latent_ids, enc_weight, dec_weight, expert_id)
        recon = recon + jnp.dot(activation, dec_part, preferred_element_type=jnp.float32)
    recon_error = (recon - rows_in.astype(jnp.float32)).astype(jnp.bfloat16)
    enc_parts = []
    dec_parts = []
    for expert_id in range(EXPERTS):
        live_mask, activation, dec_part = expert_parts(rows_in, expert_picks, latent_ids, enc_weight, dec_weight, expert_id)
        act_grad = jnp.dot(recon_error, dec_part.T, preferred_element_type=jnp.float32)
        pre_grad = jnp.where(live_mask, act_grad, jnp.float32(0.0)).astype(jnp.bfloat16)
        dec_parts.append(jnp.dot(activation.T, recon_error, preferred_element_type=jnp.float32))
        enc_parts.append(jnp.dot(rows_in.T, pre_grad, preferred_element_type=jnp.float32))
    return recon_error, jnp.concatenate(enc_parts, axis=1), jnp.concatenate(dec_parts, axis=0)
```

```python
import functools

import jax
import jax.numpy as jnp
from jax import lax
from jax.experimental import pallas as pl
from jax.experimental.pallas import tpu as pltpu
from jax.sharding import PartitionSpec as P

EXPERTS = 4
TOPK = 32
CAP = 18

STRIDE = 256
BLK = 4
META = 128
PAD = 256
MESH = pl.DeviceIdType.MESH
F32, BF16 = jnp.float32, jnp.bfloat16


def nt(a, b):
    return lax.dot_general(a, b, (((1,), (1,)), ((), ())), preferred_element_type=F32)


def nn(a, b):
    return jnp.dot(a, b, preferred_element_type=F32)


def step_kernel(
    X, Y, Z, SLOTS, TOPK,
    rows_ref, packed_ref, enc_ref, dec_ref,
    err_ref, genc_ref, gdec_ref,
    xbuf, rh, ro, eh, eo, rowst, est, enct, dech, eye, pm, pmt, offs_out, offs,
    va, vg, vact, vpre, part, sbuf, rbuf, fin, xsend, xret, errst, xerr,
    local_sem, w_send, w_recv, x_send, x_recv, m_send, m_recv, va_send, va_recv,
    vg_send, vg_recv, a_send, a_recv, b_send, b_recv, s_send, s_recv,
    r_send, r_recv, e_send, e_recv, d_send, d_recv, f_send, f_recv,
):
    p, y = lax.axis_index("expert"), lax.axis_index("chan")
    h, z, x = lax.rem(p, 2), lax.rem(p // 2, Z), p // (2 * Z)
    b, v = x * 2 + h, y * 2 + h
    nb, nv = 2 * X, 2 * Y
    rd, width = rows_ref.shape
    half, lat = width // 2, enc_ref.shape[1]
    piece, mid = half // 2, Z // 2

    def at(x_, z_, h_, y_):
        return ((x_ * Z + z_) * 2 + h_, y_)

    twin = at(x, z, 1 - h, y)

    def remote(src, dst, send, recv, to):
        return pltpu.make_async_remote_copy(
            src_ref=src, dst_ref=dst, send_sem=send, recv_sem=recv, device_id=to, device_id_type=MESH
        )

    def lanes(k):
        return pl.ds(pl.multiple_of(k * half, 128), half)

    def block(k):
        return pl.ds(pl.multiple_of(k * rd, rd), rd)

    def chunk_of(s, j):
        return lax.rem(z + (2 * j - 1) * s + Z, Z)

    barrier = pltpu.get_barrier_semaphore()
    for i in range(1, nb):
        t = lax.rem(b + i, nb)
        pl.semaphore_signal(barrier, inc=1, device_id=at(t // 2, z, lax.rem(t, 2), y), device_id_type=MESH)
    for i in range(1, Z):
        pl.semaphore_signal(barrier, inc=1, device_id=at(x, lax.rem(z + i, Z), h, y), device_id_type=MESH)
    for i in range(1, Y):
        for k in range(2):
            pl.semaphore_signal(barrier, inc=1, device_id=at(x, z, k, lax.rem(y + i, Y)), device_id_type=MESH)
    pl.semaphore_wait(barrier, nb - 1 + Z - 1 + 2 * (Y - 1))

    def x_copy(i):
        t = lax.rem(b + i, nb)
        return remote(
            packed_ref.at[lax.rem(t, 2)], xbuf.at[block(b)],
            x_send.at[i], x_recv.at[i], at(t // 2, z, lax.rem(t, 2), y),
        )

    own = [
        pltpu.make_async_copy(packed_ref.at[h], xbuf.at[block(b)], local_sem.at[0]),
        pltpu.make_async_copy(enc_ref.at[lanes(h), :], est.at[h], local_sem.at[1]),
        pltpu.make_async_copy(dec_ref.at[:, lanes(h)], dech.at[h], local_sem.at[2]),
    ]
    weights = [
        remote(enc_ref.at[lanes(1 - h), :], est.at[h], w_send.at[0], w_recv.at[0], twin),
        remote(dec_ref.at[:, lanes(1 - h)], dech.at[h], w_send.at[1], w_recv.at[1], twin),
    ]
    for i in range(1, nb):
        x_copy(i).start()
    for c in own + weights:
        c.start()

    down = lax.broadcasted_iota(jnp.int32, (PAD, PAD), 0)
    across = lax.broadcasted_iota(jnp.int32, (PAD, PAD), 1)
    eye[...] = jnp.where(down == across, 1.0, 0.0).astype(BF16)
    for buf in (rh, ro, eh, eo):
        buf[:, SLOTS:, :] = jnp.zeros((Z, PAD - SLOTS, half), BF16)
    fin[SLOTS:, :] = jnp.zeros((PAD - SLOTS, half), BF16)
    for s in range(mid + 1):
        va[s, v] = jnp.zeros((8, PAD), F32)
        vg[s, v] = jnp.zeros((8, PAD), F32)
    genc_ref[...] = jnp.zeros_like(genc_ref)
    gdec_ref[...] = jnp.zeros_like(gdec_ref)

    own[0].wait()
    for i in range(1, nb):
        x_copy(i).wait_recv()
    nr = xbuf.shape[0]
    meta_t = nt(eye[0:META, 0:META], xbuf[:, half:])
    xf = x.astype(F32)
    hit0 = meta_t[2 * TOPK : 2 * TOPK + 1] == xf
    hit1 = meta_t[2 * TOPK + 1 : 2 * TOPK + 2] == xf
    hit = jnp.where(hit0, 1.0, jnp.where(hit1, 1.0, 0.0))
    offe = jnp.where(hit0, meta_t[0:TOPK], jnp.where(hit1, meta_t[TOPK : 2 * TOPK], 0.0)).astype(BF16)
    before = jnp.where(down[0:nr, 0:nr] < across[0:nr, 0:nr], 1.0, 0.0).astype(BF16)
    rank = nn(jnp.broadcast_to(hit, (16, nr)).astype(BF16), before)[0:1]
    slot = jnp.where(hit > 0.5, rank, -1.0).astype(jnp.int32)
    pm[...] = jnp.where(down[:, 0:nr] == slot, 1.0, 0.0).astype(BF16)
    rh[z] = nn(pm[...], xbuf[:, 0:half]).astype(BF16)

    def ring_copy(buf, send, recv, s, j, q):
        c = chunk_of(s, j)
        view = buf.at[c, pl.ds(0, SLOTS), pl.ds(q * piece, piece)]
        to = at(x, lax.rem(z + (1 - 2 * j) + Z, Z), h, y)
        return remote(view, view, send.at[j, s, q], recv.at[j, s, q], to)

    def ring_wait(buf, send, recv, s, j, q):
        c = chunk_of(s, j)
        view = buf.at[c, pl.ds(0, SLOTS), pl.ds(q * piece, piece)]
        remote(view, view, send.at[j, s - 1, q], recv.at[j, s - 1, q], twin).wait_recv()

    def twin_copy(src, dst, send, recv, s, j):
        c = chunk_of(s, j)
        return remote(src.at[c, pl.ds(0, SLOTS)], dst.at[c, pl.ds(0, SLOTS)], send.at[s, j], recv.at[s, j], twin)

    def ring_step(buf, send, recv, s):
        @pl.when(jnp.logical_and(s > 0, s < mid))
        def _():
            for k in range(2):
                for j in range(2):
                    q = k if j == 0 else 1 - k
                    ring_wait(buf, send, recv, s, j, q)
                    if k == 0:
                        ring_copy(buf, send, recv, s, j, q).start()
                    else:
                        @pl.when(s < mid - 1)
                        def _():
                            ring_copy(buf, send, recv, s, j, q).start()

        @pl.when(s == mid)
        def _():
            for j in range(2):
                ring_wait(buf, send, recv, mid, j, j)

    def ring_begin(buf, send, recv):
        for k in range(2):
            for j in range(2):
                ring_copy(buf, send, recv, 0, j, k if j == 0 else 1 - k).start()

    def ring_sent(buf, send, recv):
        for s in range(mid):
            for k in range(2 if s < mid - 1 else 1):
                for j in range(2):
                    ring_copy(buf, send, recv, s, j, k if j == 0 else 1 - k).wait_send()

    def count(s):
        return jnp.where(jnp.logical_or(s == 0, s == mid), 1, 2)

    def each(s, fn):
        def body(j, carry):
            fn(j)
            return carry

        lax.fori_loop(0, count(s), body, 0)

    def value_copy(buf, send, recv, s, i):
        t = lax.rem(v + i, nv)
        return remote(
            buf.at[s, v], buf.at[s, v], send.at[s, i], recv.at[s, i], at(x, z, lax.rem(t, 2), t // 2)
        )

    def value_wait(buf, send, recv, s, i):
        view = buf.at[s, lax.rem(v - i + nv, nv)]
        remote(view, view, send.at[s, i], recv.at[s, i], twin).wait_recv()

    def live_at(c, i):
        return lax.broadcasted_iota(jnp.int32, (STRIDE, PAD), 0) == offs[c, pl.ds(i, 1), :].astype(jnp.int32)

    def partial_values(buf, weight, chunks, s, j):
        c = chunk_of(s, j)
        for i in range(BLK):
            dense = nt(weight(i), chunks[c])
            buf[s, v, pl.ds(j * BLK + i, 1), :] = jnp.sum(
                jnp.where(live_at(c, i), dense, 0.0), axis=0, keepdims=True
            )

    def whole_values(buf, send, recv, s):
        for i in range(1, nv):
            value_wait(buf, send, recv, s, i)
        total = buf[s, 0]
        for k in range(1, nv):
            total += buf[s, k]
        return total

    def spread(values, c, i):
        return jnp.where(live_at(c, i), values, 0.0).astype(BF16)

    ring_begin(rh, a_send, a_recv)

    offs_t = nt(offe, pm[...])
    for k in range(Z):
        mine = offs_t[k * BLK : (k + 1) * BLK]
        offs_out[k] = jnp.concatenate([mine, mine], axis=0)

    def meta_copy(i):
        t = lax.rem(z + i, Z)
        return remote(offs_out.at[t], offs.at[z], m_send.at[i], m_recv.at[i], at(x, t, h, y))

    for i in range(1, Z):
        meta_copy(i).start()
    offs[z] = offs_out[z]
    pmt[...] = nt(eye[0:nr, 0:nr], pm[...]).astype(BF16)

    def ro_copy(s, j):
        return twin_copy(rh, ro, d_send, d_recv, s, j)

    def eo_copy(s, j):
        return twin_copy(eh, eo, f_send, f_recv, s, j)

    own[1].wait()
    own[2].wait()
    for c in weights:
        c.wait_recv()
    for i in range(BLK):
        enct[i] = nt(eye[...], est[i // 2, :, (i % 2) * STRIDE : (i % 2 + 1) * STRIDE]).astype(BF16)
    for i in range(1, Z):
        meta_copy(i).wait_recv()

    def finish_encode(s):
        vact[s] = whole_values(va, va_send, va_recv, s)

        def decode(j):
            c = chunk_of(s, j)
            total = None
            for i in range(BLK):
                act_t = spread(vact[s, pl.ds(j * BLK + i, 1), :], c, i)
                act = nt(eye[0:SLOTS, :], act_t).astype(BF16)
                low = (i % 2) * STRIDE
                term = nn(act, dech[i // 2, low : low + STRIDE, :])
                total = term if total is None else total + term
            part[c] = total

        each(s, decode)

    def encode_step(s, carry):
        ring_step(rh, a_send, a_recv, s)
        each(s, lambda j: ro_copy(s, j).start())
        each(s, lambda j: partial_values(va, lambda i: enct[i], rh, s, j))
        for i in range(1, nv):
            value_copy(va, va_send, va_recv, s, i).start()

        @pl.when(s > 0)
        def _():
            finish_encode(s - 1)

        return carry

    lax.fori_loop(0, mid + 1, encode_step, 0)
    finish_encode(mid)

    def sum_copy(t, j, q):
        view = pl.ds(q * piece, piece)
        to = at(x, lax.rem(z + (1 - 2 * j) + Z, Z), h, y)
        return remote(
            sbuf.at[j, t - 1, :, view], rbuf.at[j, t - 1, :, view], s_send.at[j, t - 1, q], s_recv.at[j, t - 1, q], to
        )

    def transpose_rows(s):
        def one(j):
            c = chunk_of(s, j)
            ro_copy(s, j).wait_recv()
            for k, src in ((h, rh), (1 - h, ro)):
                for i in range(half // 256):
                    rowst[c, pl.ds(pl.multiple_of(k * half + i * 256, 256), 256), :] = nt(
                        eye[...], src[c, :, i * 256 : (i + 1) * 256]
                    ).astype(BF16)

        each(s, one)

    for t in range(mid, 0, -1):
        for k in range(1 if t == mid else 2):
            for j in range(2):
                q = k if j == 0 else 1 - k
                low = q * piece
                c = lax.rem(z + (1 - 2 * j) * t + Z, Z)
                total = part[c, :, low : low + piece]
                if t < mid and (t < mid - 1 or q == j):
                    sum_copy(t + 1, j, q).wait_recv()
                    total += rbuf[j, t, :, low : low + piece].astype(F32)
                sbuf[j, t - 1, :, low : low + piece] = total.astype(BF16)
                sum_copy(t, j, q).start()
        transpose_rows(jnp.int32(t))
    transpose_rows(jnp.int32(0))
    for k in range(2):
        for j in range(2):
            sum_copy(1, j, k if j == 0 else 1 - k).wait_recv()
    fin[0:SLOTS, :] = (part[z] + rbuf[0, 0].astype(F32) + rbuf[1, 0].astype(F32)).astype(BF16)

    xsend[...] = nn(pmt[...], fin[...]).astype(BF16)

    def ret_copy(i):
        t = lax.rem(b + i, nb)
        return remote(
            xsend.at[block(t)], xret.at[x, :, lanes(h)], r_send.at[i], r_recv.at[i], at(t // 2, z, lax.rem(t, 2), y)
        )

    def ret_wait(i):
        t = lax.rem(b - i + nb, nb)
        view = xret.at[t // 2, :, lanes(lax.rem(t, 2))]
        remote(view, view, r_send.at[i], r_recv.at[i], twin).wait_recv()

    for i in range(1, nb):
        ret_copy(i).start()
    xret[x, :, lanes(h)] = xsend[block(b), :]
    for i in range(1, nb):
        ret_wait(i)
    recon = xret[0].astype(F32)
    for k in range(1, X):
        recon += xret[k].astype(F32)
    error = (recon - rows_ref[...].astype(F32)).astype(BF16)
    err_ref[...] = error
    errst[...] = error

    def err_copy(i):
        t = lax.rem(b + i, nb)
        return remote(
            errst.at[:, lanes(lax.rem(t, 2))], xerr.at[block(b)],
            e_send.at[i], e_recv.at[i], at(t // 2, z, lax.rem(t, 2), y),
        )

    for i in range(1, nb):
        err_copy(i).start()
    xerr[block(b), :] = errst[:, lanes(h)]
    for i in range(1, nb):
        err_copy(i).wait_recv()
    eh[z] = nn(pm[...], xerr[...]).astype(BF16)
    ring_begin(eh, b_send, b_recv)

    def dec_block(i):
        low = (i % 2) * STRIDE
        return dech[i // 2, low : low + STRIDE, :]

    def finish_gradients(s):
        vpre[s] = whole_values(vg, vg_send, vg_recv, s)

        def accumulate(j):
            c = chunk_of(s, j)
            eo_copy(s, j).wait_recv()
            for i in range(lat // STRIDE):
                blk = h * (lat // STRIDE) + i
                row = pl.ds(j * BLK + blk, 1)
                low = i * STRIDE
                act_t = spread(vact[s, row, :], c, blk)
                pre_t = spread(vpre[s, row, :], c, blk)
                gdec_ref[low : low + STRIDE, lanes(h)] += nn(act_t, eh[c])
                gdec_ref[low : low + STRIDE, lanes(1 - h)] += nn(act_t, eo[c])
                for k in range(2):
                    part_c = slice(k * half, (k + 1) * half)
                    genc_ref[part_c, low : low + STRIDE] += nt(rowst[c, part_c, :], pre_t)

        each(s, accumulate)

    def gradient_step(s, carry):
        ring_step(eh, b_send, b_recv, s)
        each(s, lambda j: eo_copy(s, j).start())
        each(s, lambda j: partial_values(vg, dec_block, eh, s, j))
        for i in range(1, nv):
            value_copy(vg, vg_send, vg_recv, s, i).start()

        @pl.when(s > 0)
        def _():
            finish_gradients(s - 1)

        return carry

    lax.fori_loop(0, mid + 1, gradient_step, 0)
    finish_gradients(mid)

    for i in range(1, nb):
        x_copy(i).wait_send()
        ret_copy(i).wait_send()
        err_copy(i).wait_send()
    for c in weights:
        c.wait_send()
    for i in range(1, Z):
        meta_copy(i).wait_send()
    ring_sent(rh, a_send, a_recv)
    ring_sent(eh, b_send, b_recv)
    for t in range(mid, 0, -1):
        for k in range(1 if t == mid else 2):
            for j in range(2):
                sum_copy(t, j, k if j == 0 else 1 - k).wait_send()

    def sent(s, carry):
        for i in range(1, nv):
            value_copy(va, va_send, va_recv, s, i).wait_send()
            value_copy(vg, vg_send, vg_recv, s, i).wait_send()
        each(s, lambda j: ro_copy(s, j).wait_send())
        each(s, lambda j: eo_copy(s, j).wait_send())
        return carry

    lax.fori_loop(0, mid + 1, sent, 0)


def per_device(experts, topk, rows_in, expert_picks, latent_ids, enc_weight, dec_weight):
    X, Y = experts, lax.axis_size("chan")
    Z = lax.axis_size("expert") // (2 * X)
    rd, width = rows_in.shape
    lat, half, mid = enc_weight.shape[1], width // 2, Z // 2
    nb, nv = 2 * X, 2 * Y
    slots = min(-(-CAP * nb // 16) * 16, PAD) if experts == EXPERTS else PAD - 64
    blocks = jnp.arange(topk, dtype=jnp.int32) * STRIDE
    meta = jnp.concatenate(
        [
            (latent_ids - blocks[None, None, :]).reshape(rd, 2 * topk),
            expert_picks,
            jnp.zeros((rd, META - 2 * topk - 2), jnp.int32),
        ],
        axis=1,
    ).astype(BF16)
    packed = jnp.stack(
        [jnp.concatenate([rows_in[:, k * half : (k + 1) * half], meta], axis=1) for k in range(2)]
    )
    vmem, anywhere = pl.BlockSpec(memory_space=pltpu.VMEM), pl.BlockSpec(memory_space=pl.ANY)
    dma = pltpu.SemaphoreType.DMA
    scratch = [
        pltpu.VMEM((nb * rd, half + META), BF16),
        pltpu.VMEM((Z, PAD, half), BF16),
        pltpu.VMEM((Z, PAD, half), BF16),
        pltpu.VMEM((Z, PAD, half), BF16),
        pltpu.VMEM((Z, PAD, half), BF16),
        pltpu.VMEM((Z, width, PAD), BF16),
        pltpu.VMEM((2, half, lat), BF16),
        pltpu.VMEM((BLK, STRIDE, half), BF16),
        pltpu.VMEM((2, lat, half), BF16),
        pltpu.VMEM((PAD, PAD), BF16),
        pltpu.VMEM((PAD, nb * rd), BF16),
        pltpu.VMEM((nb * rd, PAD), BF16),
        pltpu.VMEM((Z, 8, PAD), F32),
        pltpu.VMEM((Z, 8, PAD), F32),
        pltpu.VMEM((mid + 1, nv, 8, PAD), F32),
        pltpu.VMEM((mid + 1, nv, 8, PAD), F32),
        pltpu.VMEM((mid + 1, 8, PAD), F32),
        pltpu.VMEM((mid + 1, 8, PAD), F32),
        pltpu.VMEM((Z, slots, half), F32),
        pltpu.VMEM((2, mid, slots, half), BF16),
        pltpu.VMEM((2, mid, slots, half), BF16),
        pltpu.VMEM((PAD, half), BF16),
        pltpu.VMEM((nb * rd, half), BF16),
        pltpu.VMEM((X, rd, width), BF16),
        pltpu.VMEM((rd, width), BF16),
        pltpu.VMEM((nb * rd, half), BF16),
        dma((3,)),
    ]
    pairs = [(2,), (nb,), (Z,), (mid + 1, nv), (mid + 1, nv), (2, mid, 2), (2, mid, 2), (2, mid, 2)]
    pairs += [(nb,), (nb,), (mid + 1, 2), (mid + 1, 2)]
    for shape in pairs:
        scratch += [dma(shape), dma(shape)]
    return pl.pallas_call(
        functools.partial(step_kernel, X, Y, Z, slots, topk),
        out_shape=(
            jax.ShapeDtypeStruct(rows_in.shape, BF16),
            jax.ShapeDtypeStruct(enc_weight.shape, F32),
            jax.ShapeDtypeStruct(dec_weight.shape, F32),
        ),
        in_specs=[vmem, anywhere, anywhere, anywhere],
        out_specs=(vmem, vmem, vmem),
        scratch_shapes=scratch,
        compiler_params=pltpu.CompilerParams(
            collective_id=0, has_side_effects=True, vmem_limit_bytes=60 * 2**20
        ),
    )(rows_in, packed, enc_weight, dec_weight)


def solution(mesh, experts=EXPERTS, topk=TOPK):
    placed = (
        P("expert", "chan"),
        P("expert", None),
        P("expert", None, None),
        P("chan", "expert"),
        P("expert", "chan"),
    )
    return jax.shard_map(
        functools.partial(per_device, experts, topk),
        mesh=mesh,
        in_specs=placed,
        out_specs=(P("expert", "chan"), P("chan", "expert"), P("expert", "chan")),
        check_vma=False,
    )
```

```python
import functools

import jax
import jax.numpy as jnp
from jax import lax
from jax.experimental import pallas as pl
from jax.experimental.pallas import tpu as pltpu
from jax.sharding import PartitionSpec as P

EXPERTS = 4
TOPK = 32
CAP = 18

STRIDE = 256
BLK = 4
META = 128
PAD = 256
MESH = pl.DeviceIdType.MESH
F32, BF16 = jnp.float32, jnp.bfloat16


def nt(a, b):
    return lax.dot_general(a, b, (((1,), (1,)), ((), ())), preferred_element_type=F32)


def nn(a, b):
    return jnp.dot(a, b, preferred_element_type=F32)


def step_kernel(
    X, Y, Z, SLOTS, TOPK,
    rows_ref, picks_ref, ids_ref, enc_ref, dec_ref,
    err_ref, genc_ref, gdec_ref,
    packed_ref, xbuf, rh, ro, eh, eo, rowst, est, enct, dech, eye, pm, pmt, offs_out, offs,
    va, vg, vact, vpre, part, sbuf, rbuf, fin, xsend, xret, xerr,
    local_sem, w_send, w_recv, x_send, x_recv, m_send, m_recv, va_send, va_recv,
    vg_send, vg_recv, a_send, a_recv, b_send, b_recv, s_send, s_recv,
    r_send, r_recv, e_send, e_recv, d_send, d_recv, f_send, f_recv,
):
    p, y = lax.axis_index("expert"), lax.axis_index("chan")
    h, z, x = lax.rem(p, 2), lax.rem(p // 2, Z), p // (2 * Z)
    b, v = x * 2 + h, y * 2 + h
    nb, nv = 2 * X, 2 * Y
    rd, width = rows_ref.shape
    half, lat = width // 2, enc_ref.shape[1]
    piece, mid = half // 2, Z // 2

    def at(x_, z_, h_, y_):
        return ((x_ * Z + z_) * 2 + h_, y_)

    twin = at(x, z, 1 - h, y)

    def remote(src, dst, send, recv, to):
        return pltpu.make_async_remote_copy(
            src_ref=src, dst_ref=dst, send_sem=send, recv_sem=recv, device_id=to, device_id_type=MESH
        )

    def lanes(k):
        return pl.ds(pl.multiple_of(k * half, 128), half)

    def block(k):
        return pl.ds(pl.multiple_of(k * rd, rd), rd)

    def chunk_of(s, j):
        return lax.rem(z + (2 * j - 1) * s + Z, Z)

    barrier = pltpu.get_barrier_semaphore()
    for i in range(1, nb):
        t = lax.rem(b + i, nb)
        pl.semaphore_signal(barrier, inc=1, device_id=at(t // 2, z, lax.rem(t, 2), y), device_id_type=MESH)
    for i in range(1, Z):
        pl.semaphore_signal(barrier, inc=1, device_id=at(x, lax.rem(z + i, Z), h, y), device_id_type=MESH)
    for i in range(1, Y):
        for k in range(2):
            pl.semaphore_signal(barrier, inc=1, device_id=at(x, z, k, lax.rem(y + i, Y)), device_id_type=MESH)
    for k in range(2):
        packed_ref[k, :, 0:half] = rows_ref[:, k * half : (k + 1) * half]
    starts = lax.broadcasted_iota(jnp.int32, (rd, TOPK), 1) * STRIDE
    first = lax.broadcasted_iota(jnp.int32, (16, rd), 0) == 0
    picked = jnp.where(first, picks_ref[0:1, :], picks_ref[1:2, :]).astype(F32).astype(BF16)
    small = lax.broadcasted_iota(jnp.int32, (rd, rd), 0) == lax.broadcasted_iota(jnp.int32, (rd, rd), 1)
    pick_columns = nt(jnp.where(small, 1.0, 0.0).astype(BF16), picked)
    meta = jnp.concatenate(
        [(ids_ref[:, k, :] - starts).astype(F32) for k in range(2)]
        + [pick_columns, jnp.zeros((rd, META - 2 * TOPK - 16), F32)],
        axis=1,
    ).astype(BF16)
    for k in range(2):
        packed_ref[k, :, half:] = meta
    down = lax.broadcasted_iota(jnp.int32, (PAD, PAD), 0)
    across = lax.broadcasted_iota(jnp.int32, (PAD, PAD), 1)
    eye[...] = jnp.where(down == across, 1.0, 0.0).astype(BF16)
    for buf in (rh, ro, eh, eo):
        buf[:, SLOTS:, :] = jnp.zeros((Z, PAD - SLOTS, half), BF16)
    fin[SLOTS:, :] = jnp.zeros((PAD - SLOTS, half), BF16)
    for s in range(mid + 1):
        va[s, v] = jnp.zeros((8, PAD), F32)
        vg[s, v] = jnp.zeros((8, PAD), F32)
    genc_ref[...] = jnp.zeros_like(genc_ref)
    gdec_ref[...] = jnp.zeros_like(gdec_ref)

    pl.semaphore_wait(barrier, nb - 1 + Z - 1 + 2 * (Y - 1))

    def x_copy(i):
        t = lax.rem(b + i, nb)
        return remote(
            packed_ref.at[lax.rem(t, 2)], xbuf.at[block(b)],
            x_send.at[i], x_recv.at[i], at(t // 2, z, lax.rem(t, 2), y),
        )

    own = [
        pltpu.make_async_copy(packed_ref.at[h], xbuf.at[block(b)], local_sem.at[0]),
        pltpu.make_async_copy(enc_ref.at[lanes(h), :], est.at[h], local_sem.at[1]),
        pltpu.make_async_copy(dec_ref.at[:, lanes(h)], dech.at[h], local_sem.at[2]),
    ]
    weights = [
        remote(enc_ref.at[lanes(1 - h), :], est.at[h], w_send.at[0], w_recv.at[0], twin),
        remote(dec_ref.at[:, lanes(1 - h)], dech.at[h], w_send.at[1], w_recv.at[1], twin),
    ]
    for i in range(1, nb):
        x_copy(i).start()
    for c in own + weights:
        c.start()

    def turn_encoder(k):
        for i in range(lat // STRIDE):
            enct[k * (lat // STRIDE) + i] = nt(
                eye[...], est[k, :, i * STRIDE : (i + 1) * STRIDE]
            ).astype(BF16)

    own[1].wait()
    turn_encoder(h)
    own[0].wait()
    for i in range(1, nb):
        x_copy(i).wait_recv()
    nr = xbuf.shape[0]
    meta_t = nt(eye[0:META, 0:META], xbuf[:, half:])
    xf = x.astype(F32)
    hit0 = meta_t[2 * TOPK : 2 * TOPK + 1] == xf
    hit1 = meta_t[2 * TOPK + 1 : 2 * TOPK + 2] == xf
    hit = jnp.where(hit0, 1.0, jnp.where(hit1, 1.0, 0.0))
    offe = jnp.where(hit0, meta_t[0:TOPK], jnp.where(hit1, meta_t[TOPK : 2 * TOPK], 0.0)).astype(BF16)
    before = jnp.where(down[0:nr, 0:nr] < across[0:nr, 0:nr], 1.0, 0.0).astype(BF16)
    rank = nn(jnp.broadcast_to(hit, (16, nr)).astype(BF16), before)[0:1]
    slot = jnp.where(hit > 0.5, rank, -1.0).astype(jnp.int32)
    pm[...] = jnp.where(down[:, 0:nr] == slot, 1.0, 0.0).astype(BF16)
    rh[z] = nn(pm[...], xbuf[:, 0:half]).astype(BF16)

    def ring_copy(buf, send, recv, s, j, q):
        c = chunk_of(s, j)
        view = buf.at[c, pl.ds(0, SLOTS), pl.ds(q * piece, piece)]
        to = at(x, lax.rem(z + (1 - 2 * j) + Z, Z), h, y)
        return remote(view, view, send.at[j, s, q], recv.at[j, s, q], to)

    def ring_wait(buf, send, recv, s, j, q):
        c = chunk_of(s, j)
        view = buf.at[c, pl.ds(0, SLOTS), pl.ds(q * piece, piece)]
        remote(view, view, send.at[j, s - 1, q], recv.at[j, s - 1, q], twin).wait_recv()

    def twin_copy(src, dst, send, recv, s, j):
        c = chunk_of(s, j)
        return remote(src.at[c, pl.ds(0, SLOTS)], dst.at[c, pl.ds(0, SLOTS)], send.at[s, j], recv.at[s, j], twin)

    def order(swap, j, k):
        return 1 - k if swap and j == 1 else k

    def ring_pass(buf, send, recv, s, k, swap):
        for j in range(2):
            q = order(swap, j, k)
            ring_wait(buf, send, recv, s, j, q)
            if q == j:
                ring_copy(buf, send, recv, s, j, q).start()
            else:
                @pl.when(s < mid - 1)
                def _():
                    ring_copy(buf, send, recv, s, j, q).start()

    def ring_begin(buf, send, recv, k, swap):
        for j in range(2):
            ring_copy(buf, send, recv, 0, j, order(swap, j, k)).start()

    def ring_end(buf, send, recv):
        for j in range(2):
            ring_wait(buf, send, recv, mid, j, j)

    def ring_sent(buf, send, recv):
        for s in range(mid):
            for j in range(2):
                for q in range(2):
                    if s < mid - 1 or q == j:
                        ring_copy(buf, send, recv, s, j, q).wait_send()

    def sides(s):
        return (0,) if isinstance(s, int) and s in (0, mid) else (0, 1)

    def value_copy(buf, send, recv, s, i):
        t = lax.rem(v + i, nv)
        return remote(
            buf.at[s, v], buf.at[s, v], send.at[s, i], recv.at[s, i], at(x, z, lax.rem(t, 2), t // 2)
        )

    def value_wait(buf, send, recv, s, i):
        view = buf.at[s, lax.rem(v - i + nv, nv)]
        remote(view, view, send.at[s, i], recv.at[s, i], twin).wait_recv()

    def live_at(c, i):
        return lax.broadcasted_iota(jnp.int32, (STRIDE, PAD), 0) == offs[c, pl.ds(i, 1), :].astype(jnp.int32)

    def partial_values(buf, send, recv, weight, chunks, s):
        for j in sides(s):
            c = chunk_of(s, j)
            for i in range(BLK):
                dense = nt(weight(i), chunks[c])
                buf[s, v, j * BLK + i : j * BLK + i + 1, :] = jnp.sum(
                    jnp.where(live_at(c, i), dense, 0.0), axis=0, keepdims=True
                )
        for i in range(1, nv):
            value_copy(buf, send, recv, s, i).start()

    def whole_values(buf, send, recv, s):
        for i in range(1, nv):
            value_wait(buf, send, recv, s, i)
        total = buf[s, 0]
        for k in range(1, nv):
            total += buf[s, k]
        return total

    def spread(values, c, i):
        return jnp.where(live_at(c, i), values, 0.0).astype(BF16)

    for k in range(2):
        ring_begin(rh, a_send, a_recv, k, True)

    offs_t = nt(offe, pm[...])
    for k in range(Z):
        mine = offs_t[k * BLK : (k + 1) * BLK]
        offs_out[k] = jnp.concatenate([mine, mine], axis=0)

    def meta_copy(i):
        t = lax.rem(z + i, Z)
        return remote(offs_out.at[t], offs.at[z], m_send.at[i], m_recv.at[i], at(x, t, h, y))

    for i in range(1, Z):
        meta_copy(i).start()
    offs[z] = offs_out[z]

    def ro_copy(s, j):
        return twin_copy(rh, ro, d_send, d_recv, s, j)

    def eo_copy(s, j):
        return twin_copy(eh, eo, f_send, f_recv, s, j)

    def encode(s):
        for j in sides(s):
            ro_copy(s, j).start()
        partial_values(va, va_send, va_recv, lambda i: enct[i], rh, s)

    def decode(s):
        vact[s] = whole_values(va, va_send, va_recv, s)
        for j in sides(s):
            c = chunk_of(s, j)
            total = None
            for i in range(BLK):
                act_t = spread(vact[s, j * BLK + i : j * BLK + i + 1, :], c, i)
                act = nt(eye[0:SLOTS, :], act_t).astype(BF16)
                term = nn(act, dec_block(i))
                total = term if total is None else total + term
            part[c] = total

    def dec_block(i):
        low = (i % 2) * STRIDE
        return dech[i // 2, low : low + STRIDE, :]

    for c in weights:
        c.wait_recv()
    turn_encoder(1 - h)
    own[2].wait()
    encode(0)
    for i in range(1, Z):
        meta_copy(i).wait_recv()

    def encode_step(s, carry):
        ring_pass(rh, a_send, a_recv, s, 0, True)

        @pl.when(s == 2)
        def _():
            decode(0)

        @pl.when(s > 2)
        def _():
            decode(s - 2)

        ring_pass(rh, a_send, a_recv, s, 1, True)
        encode(s)
        return carry

    lax.fori_loop(1, mid, encode_step, 0)
    decode(mid - 2)
    ring_end(rh, a_send, a_recv)
    encode(mid)
    decode(mid - 1)

    def sum_copy(t, j, q):
        view = pl.ds(q * piece, piece)
        to = at(x, lax.rem(z + (1 - 2 * j) + Z, Z), h, y)
        return remote(
            sbuf.at[j, t - 1, :, view], rbuf.at[j, t - 1, :, view], s_send.at[j, t - 1, q], s_recv.at[j, t - 1, q], to
        )

    def transpose_rows(s):
        for j in sides(s):
            c = chunk_of(s, j)
            ro_copy(s, j).wait_recv()
            for k, src in ((h, rh), (1 - h, ro)):
                for i in range(half // 256):
                    rowst[c, pl.ds(pl.multiple_of(k * half + i * 256, 256), 256), :] = nt(
                        eye[...], src[c, :, i * 256 : (i + 1) * 256]
                    ).astype(BF16)

    def sum_step(t, k):
        for j in range(2):
            q = order(True, j, k)
            low = q * piece
            c = chunk_of(t, 1 - j)
            total = part[c, :, low : low + piece]
            if t < mid - 1 or (t < mid and q == j):
                sum_copy(t + 1, j, q).wait_recv()
                total += rbuf[j, t, :, low : low + piece].astype(F32)
            sbuf[j, t - 1, :, low : low + piece] = total.astype(BF16)
            sum_copy(t, j, q).start()

    sum_step(mid - 1, 1)
    decode(mid)
    sum_step(mid, 0)
    sum_step(mid - 1, 0)
    pmt[...] = nt(eye[0:nr, 0:nr], pm[...]).astype(BF16)
    transpose_rows(0)
    for t in range(mid - 2, 0, -1):
        sum_step(t, 1)
        transpose_rows(t)
        sum_step(t, 0)
    transpose_rows(mid - 1)
    transpose_rows(mid)

    def part_lanes(k, q):
        return pl.ds(pl.multiple_of(k * half + q * piece, 128), piece)

    def ret_copy(i, q):
        t = lax.rem(b + i, nb)
        return remote(
            xsend.at[block(t), pl.ds(q * piece, piece)], xret.at[x, :, part_lanes(h, q)],
            r_send.at[i, q], r_recv.at[i, q], at(t // 2, z, lax.rem(t, 2), y),
        )

    def ret_wait(i, q):
        t = lax.rem(b - i + nb, nb)
        view = xret.at[t // 2, :, part_lanes(lax.rem(t, 2), q)]
        remote(view, view, r_send.at[i, q], r_recv.at[i, q], twin).wait_recv()

    def err_copy(i, q):
        t = lax.rem(b + i, nb)
        return remote(
            err_ref.at[:, part_lanes(lax.rem(t, 2), q)], xerr.at[block(b), pl.ds(q * piece, piece)],
            e_send.at[i, q], e_recv.at[i, q], at(t // 2, z, lax.rem(t, 2), y),
        )

    for q in range(2):
        own_lanes = slice(q * piece, (q + 1) * piece)
        for j in range(2):
            sum_copy(1, j, q).wait_recv()
        fin[0:SLOTS, own_lanes] = (
            part[z, :, own_lanes] + rbuf[0, 0, :, own_lanes].astype(F32) + rbuf[1, 0, :, own_lanes].astype(F32)
        ).astype(BF16)
        xsend[:, own_lanes] = nn(pmt[...], fin[:, own_lanes]).astype(BF16)
        for i in range(1, nb):
            ret_copy(i, q).start()
        xret[x, :, part_lanes(h, q)] = xsend[block(b), own_lanes]

    for q in range(2):
        for i in range(1, nb):
            ret_wait(i, q)
        for k in range(2):
            cols = slice(k * half + q * piece, k * half + (q + 1) * piece)
            recon = xret[0, :, cols].astype(F32)
            for e in range(1, X):
                recon += xret[e, :, cols].astype(F32)
            err_ref[:, cols] = (recon - rows_ref[:, cols].astype(F32)).astype(BF16)
        for i in range(1, nb):
            err_copy(i, q).start()
        xerr[block(b), q * piece : (q + 1) * piece] = err_ref[:, part_lanes(h, q)]

    for q in range(2):
        for i in range(1, nb):
            err_copy(i, q).wait_recv()
        eh[z, :, q * piece : (q + 1) * piece] = nn(pm[...], xerr[:, q * piece : (q + 1) * piece]).astype(BF16)
        ring_begin(eh, b_send, b_recv, q, False)

    def latent_grads(s):
        for j in sides(s):
            eo_copy(s, j).start()
        partial_values(vg, vg_send, vg_recv, dec_block, eh, s)

    def add_dec(s):
        for j in sides(s):
            eo_copy(s, j).wait_recv()
        for i in range(lat // STRIDE):
            blk = h * (lat // STRIDE) + i
            low = i * STRIDE
            acts = [(chunk_of(s, j), spread(vact[s, pl.ds(j * BLK + blk, 1), :], chunk_of(s, j), blk)) for j in sides(s)]
            for k, src in ((h, eh), (1 - h, eo)):
                gdec_ref[low : low + STRIDE, lanes(k)] += sum(nn(a, src[c]) for c, a in acts)

    def add_enc(s):
        vpre[s] = whole_values(vg, vg_send, vg_recv, s)
        for i in range(lat // STRIDE):
            blk = h * (lat // STRIDE) + i
            low = i * STRIDE
            pres = [(chunk_of(s, j), spread(vpre[s, pl.ds(j * BLK + blk, 1), :], chunk_of(s, j), blk)) for j in sides(s)]
            for k in range(2):
                cols = slice(k * half, (k + 1) * half)
                genc_ref[cols, low : low + STRIDE] += sum(nt(rowst[c, cols, :], g) for c, g in pres)

    latent_grads(0)

    def gradient_step(s, carry):
        ring_pass(eh, b_send, b_recv, s, 0, False)

        @pl.when(s == 1)
        def _():
            add_dec(0)

        @pl.when(s == 2)
        def _():
            add_enc(0)

        @pl.when(s > 2)
        def _():
            add_enc(s - 2)

        ring_pass(eh, b_send, b_recv, s, 1, False)
        latent_grads(s)

        @pl.when(s > 1)
        def _():
            add_dec(s - 1)

        return carry

    lax.fori_loop(1, mid, gradient_step, 0)
    add_enc(mid - 2)
    ring_end(eh, b_send, b_recv)
    latent_grads(mid)
    add_dec(mid - 1)
    add_enc(mid - 1)
    add_dec(mid)
    add_enc(mid)

    for i in range(1, nb):
        x_copy(i).wait_send()
        for q in range(2):
            ret_copy(i, q).wait_send()
            err_copy(i, q).wait_send()
    for c in weights:
        c.wait_send()
    for i in range(1, Z):
        meta_copy(i).wait_send()
    ring_sent(rh, a_send, a_recv)
    ring_sent(eh, b_send, b_recv)
    for t in range(mid, 0, -1):
        for j in range(2):
            for q in range(2):
                if t < mid or q == j:
                    sum_copy(t, j, q).wait_send()

    def sent(s):
        for i in range(1, nv):
            value_copy(va, va_send, va_recv, s, i).wait_send()
            value_copy(vg, vg_send, vg_recv, s, i).wait_send()
        for j in sides(s):
            ro_copy(s, j).wait_send()
            eo_copy(s, j).wait_send()

    def sent_step(s, carry):
        sent(s)
        return carry

    sent(0)
    lax.fori_loop(1, mid, sent_step, 0)
    sent(mid)


def per_device(experts, topk, cap, rows_in, expert_picks, latent_ids, enc_weight, dec_weight):
    X, Y = experts, lax.axis_size("chan")
    Z = lax.axis_size("expert") // (2 * X)
    rd, width = rows_in.shape
    lat, half, mid = enc_weight.shape[1], width // 2, Z // 2
    nb, nv = 2 * X, 2 * Y
    slots = min(-(-cap * nb // 16) * 16, PAD)
    vmem, anywhere = pl.BlockSpec(memory_space=pltpu.VMEM), pl.BlockSpec(memory_space=pl.ANY)
    dma = pltpu.SemaphoreType.DMA
    scratch = [
        pltpu.VMEM((2, rd, half + META), BF16),
        pltpu.VMEM((nb * rd, half + META), BF16),
        pltpu.VMEM((Z, PAD, half), BF16),
        pltpu.VMEM((Z, PAD, half), BF16),
        pltpu.VMEM((Z, PAD, half), BF16),
        pltpu.VMEM((Z, PAD, half), BF16),
        pltpu.VMEM((Z, width, PAD), BF16),
        pltpu.VMEM((2, half, lat), BF16),
        pltpu.VMEM((BLK, STRIDE, half), BF16),
        pltpu.VMEM((2, lat, half), BF16),
        pltpu.VMEM((PAD, PAD), BF16),
        pltpu.VMEM((PAD, nb * rd), BF16),
        pltpu.VMEM((nb * rd, PAD), BF16),
        pltpu.VMEM((Z, 8, PAD), F32),
        pltpu.VMEM((Z, 8, PAD), F32),
        pltpu.VMEM((mid + 1, nv, 8, PAD), F32),
        pltpu.VMEM((mid + 1, nv, 8, PAD), F32),
        pltpu.VMEM((mid + 1, 8, PAD), F32),
        pltpu.VMEM((mid + 1, 8, PAD), F32),
        pltpu.VMEM((Z, slots, half), F32),
        pltpu.VMEM((2, mid, slots, half), BF16),
        pltpu.VMEM((2, mid, slots, half), BF16),
        pltpu.VMEM((PAD, half), BF16),
        pltpu.VMEM((nb * rd, half), BF16),
        pltpu.VMEM((X, rd, width), BF16),
        pltpu.VMEM((nb * rd, half), BF16),
        dma((3,)),
    ]
    pairs = [(2,), (nb,), (Z,), (mid + 1, nv), (mid + 1, nv), (2, mid, 2), (2, mid, 2), (2, mid, 2)]
    pairs += [(nb, 2), (nb, 2), (mid + 1, 2), (mid + 1, 2)]
    for shape in pairs:
        scratch += [dma(shape), dma(shape)]
    return pl.pallas_call(
        functools.partial(step_kernel, X, Y, Z, slots, topk),
        out_shape=(
            pltpu.VMEM(rows_in.shape, BF16),
            pltpu.VMEM(enc_weight.shape, F32),
            pltpu.VMEM(dec_weight.shape, F32),
        ),
        in_specs=[vmem, vmem, vmem, anywhere, anywhere],
        out_specs=(vmem, vmem, vmem),
        scratch_shapes=scratch,
        compiler_params=pltpu.CompilerParams(
            collective_id=0, has_side_effects=True, vmem_limit_bytes=46 * 2**20
        ),
    )(rows_in, expert_picks.T, latent_ids, enc_weight, dec_weight)


def solution(mesh, experts=EXPERTS, topk=TOPK, cap=CAP):
    placed = (
        P("expert", "chan"),
        P("expert", None),
        P("expert", None, None),
        P("chan", "expert"),
        P("expert", "chan"),
    )
    return jax.shard_map(
        functools.partial(per_device, experts, topk, cap),
        mesh=mesh,
        in_specs=placed,
        out_specs=(P("expert", "chan"), P("chan", "expert"), P("expert", "chan")),
        check_vma=False,
    )
```

```python
import functools

import jax
import jax.numpy as jnp
from jax import lax
from jax.experimental import pallas as pl
from jax.experimental.pallas import tpu as pltpu
from jax.sharding import PartitionSpec as P

EXPERTS = 4
TOPK = 32
CAP = 18

STRIDE = 256
BLK = 4
META = 128
PAD = 256
MESH = pl.DeviceIdType.MESH
F32, BF16 = jnp.float32, jnp.bfloat16


def nt(a, b):
    return lax.dot_general(a, b, (((1,), (1,)), ((), ())), preferred_element_type=F32)


def nn(a, b):
    return jnp.dot(a, b, preferred_element_type=F32)


def step_kernel(
    X, Y, Z, SLOTS, TOPK,
    rows_hbm, picks_hbm, ids_hbm, enc_ref, dec_ref,
    err_ref, genc_ref, gdec_ref,
    rows_ref, picks_ref, ids_ref, meta_ref, xmeta, xbuf, rh, ro, eh, eo, rowst, est, enct, dech, eye, pm, pmt, offs_out, offs,
    va, vg, vact, vpre, part, sbuf, rbuf, fin, xsend, xret, xerr,
    local_sem, q_send, q_recv, w_send, w_recv, x_send, x_recv, m_send, m_recv, va_send, va_recv,
    vg_send, vg_recv, a_send, a_recv, b_send, b_recv, s_send, s_recv,
    r_send, r_recv, e_send, e_recv, d_send, d_recv, f_send, f_recv,
):
    p, y = lax.axis_index("expert"), lax.axis_index("chan")
    h, z, x = lax.rem(p, 2), lax.rem(p // 2, Z), p // (2 * Z)
    b, v = x * 2 + h, y * 2 + h
    nb, nv = 2 * X, 2 * Y
    rd, width = rows_ref.shape
    half, lat = width // 2, enc_ref.shape[1]
    piece, mid = half // 2, Z // 2

    def at(x_, z_, h_, y_):
        return ((x_ * Z + z_) * 2 + h_, y_)

    twin = at(x, z, 1 - h, y)

    def remote(src, dst, send, recv, to):
        return pltpu.make_async_remote_copy(
            src_ref=src, dst_ref=dst, send_sem=send, recv_sem=recv, device_id=to, device_id_type=MESH
        )

    def lanes(k):
        return pl.ds(pl.multiple_of(k * half, 128), half)

    def block(k):
        return pl.ds(pl.multiple_of(k * rd, rd), rd)

    def chunk_of(s, j):
        return lax.rem(z + (2 * j - 1) * s + Z, Z)

    small_in = [
        pltpu.make_async_copy(src, dst, local_sem.at[3 + n])
        for n, (src, dst) in enumerate(((rows_hbm, rows_ref), (picks_hbm, picks_ref), (ids_hbm, ids_ref)))
    ]
    for c in small_in:
        c.start()

    barrier = pltpu.get_barrier_semaphore()
    for i in range(1, nb):
        t = lax.rem(b + i, nb)
        pl.semaphore_signal(barrier, inc=1, device_id=at(t // 2, z, lax.rem(t, 2), y), device_id_type=MESH)
    for i in range(1, Z):
        pl.semaphore_signal(barrier, inc=1, device_id=at(x, lax.rem(z + i, Z), h, y), device_id_type=MESH)
    for i in range(1, Y):
        for k in range(2):
            pl.semaphore_signal(barrier, inc=1, device_id=at(x, z, k, lax.rem(y + i, Y)), device_id_type=MESH)
    down = lax.broadcasted_iota(jnp.int32, (PAD, PAD), 0)
    across = lax.broadcasted_iota(jnp.int32, (PAD, PAD), 1)
    eye[...] = jnp.where(down == across, 1.0, 0.0).astype(BF16)
    for buf in (rh, ro, eh, eo):
        buf[:, SLOTS:, :] = jnp.zeros((Z, PAD - SLOTS, half), BF16)
    fin[SLOTS:, :] = jnp.zeros((PAD - SLOTS, half), BF16)
    for s in range(mid + 1):
        va[s, v] = jnp.zeros((8, PAD), F32)
        vg[s, v] = jnp.zeros((8, PAD), F32)
    genc_ref[...] = jnp.zeros_like(genc_ref)
    gdec_ref[...] = jnp.zeros_like(gdec_ref)

    for c in small_in:
        c.wait()
    starts = lax.broadcasted_iota(jnp.int32, (rd, TOPK), 1) * STRIDE
    first = lax.broadcasted_iota(jnp.int32, (16, rd), 0) == 0
    picked = jnp.where(first, picks_ref[0:1, :], picks_ref[1:2, :]).astype(F32).astype(BF16)
    small = lax.broadcasted_iota(jnp.int32, (rd, rd), 0) == lax.broadcasted_iota(jnp.int32, (rd, rd), 1)
    pick_columns = nt(jnp.where(small, 1.0, 0.0).astype(BF16), picked)
    meta_ref[...] = jnp.concatenate(
        [(ids_ref[:, k, :] - starts).astype(F32) for k in range(2)]
        + [pick_columns, jnp.zeros((rd, META - 2 * TOPK - 16), F32)],
        axis=1,
    ).astype(BF16)
    xmeta[block(b), :] = meta_ref[...]
    xbuf[block(b), :] = rows_ref[:, lanes(h)]
    pl.semaphore_wait(barrier, nb - 1 + Z - 1 + 2 * (Y - 1))

    def part_lanes(k, q):
        return pl.ds(pl.multiple_of(k * half + q * piece, 128), piece)

    def near(i):
        t = lax.rem(b + i, nb)
        return lax.rem(t, 2), at(t // 2, z, lax.rem(t, 2), y)

    def route_copy(i):
        _, to = near(i)
        return remote(meta_ref, xmeta.at[block(b)], q_send.at[i], q_recv.at[i], to)

    def x_copy(i, q):
        k, to = near(i)
        return remote(
            rows_ref.at[:, part_lanes(k, q)], xbuf.at[block(b), pl.ds(q * piece, piece)],
            x_send.at[i, q], x_recv.at[i, q], to,
        )

    mine = pl.ds(pl.multiple_of(h * lat, lat), lat)
    own = [
        pltpu.make_async_copy(enc_ref.at[lanes(h), :], est.at[h], local_sem.at[0]),
        pltpu.make_async_copy(dec_ref.at[:, lanes(h)], dech.at[mine], local_sem.at[1]),
    ]
    weights = [
        remote(enc_ref.at[lanes(1 - h), :], est.at[h], w_send.at[0], w_recv.at[0], twin),
        remote(dec_ref.at[:, lanes(1 - h)], dech.at[mine], w_send.at[1], w_recv.at[1], twin),
    ]
    for i in range(1, nb):
        route_copy(i).start()
    for q in range(2):
        for i in range(1, nb):
            x_copy(i, q).start()
    for c in own + weights:
        c.start()

    def turn_encoder(k):
        for i in range(lat // STRIDE):
            low = pl.multiple_of(k * lat + i * STRIDE, STRIDE)
            enct[pl.ds(low, STRIDE), :] = nt(
                eye[...], est[k, :, i * STRIDE : (i + 1) * STRIDE]
            ).astype(BF16)

    for i in range(1, nb):
        route_copy(i).wait_recv()
    nr = xbuf.shape[0]
    meta_t = nt(eye[0:META, 0:META], xmeta[...])
    xf = x.astype(F32)
    hit0 = meta_t[2 * TOPK : 2 * TOPK + 1] == xf
    hit1 = meta_t[2 * TOPK + 1 : 2 * TOPK + 2] == xf
    hit = jnp.where(hit0, 1.0, jnp.where(hit1, 1.0, 0.0))
    offe = jnp.where(hit0, meta_t[0:TOPK], jnp.where(hit1, meta_t[TOPK : 2 * TOPK], 0.0)).astype(BF16)
    before = jnp.where(down[0:nr, 0:nr] < across[0:nr, 0:nr], 1.0, 0.0).astype(BF16)
    rank = nn(jnp.broadcast_to(hit, (16, nr)).astype(BF16), before)[0:1]
    slot = jnp.where(hit > 0.5, rank, -1.0).astype(jnp.int32)
    pm[...] = jnp.where(down[:, 0:nr] == slot, 1.0, 0.0).astype(BF16)
    offs_t = nt(offe, pm[...])
    for k in range(Z):
        mine = offs_t[k * BLK : (k + 1) * BLK]
        offs_out[k] = jnp.concatenate([mine, mine], axis=0)

    def meta_copy(i):
        t = lax.rem(z + i, Z)
        return remote(offs_out.at[t], offs.at[z], m_send.at[i], m_recv.at[i], at(x, t, h, y))

    for i in range(1, Z):
        meta_copy(i).start()
    offs[z] = offs_out[z]
    own[0].wait()
    turn_encoder(h)

    def ring_copy(buf, send, recv, s, j, q):
        c = chunk_of(s, j)
        view = buf.at[c, pl.ds(0, SLOTS), pl.ds(q * piece, piece)]
        to = at(x, lax.rem(z + (1 - 2 * j) + Z, Z), h, y)
        return remote(view, view, send.at[j, s, q], recv.at[j, s, q], to)

    def ring_wait(buf, send, recv, s, j, q):
        c = chunk_of(s, j)
        view = buf.at[c, pl.ds(0, SLOTS), pl.ds(q * piece, piece)]
        remote(view, view, send.at[j, s - 1, q], recv.at[j, s - 1, q], twin).wait_recv()

    def twin_copy(src, dst, send, recv, s, j):
        c = chunk_of(s, j)
        return remote(src.at[c, pl.ds(0, SLOTS)], dst.at[c, pl.ds(0, SLOTS)], send.at[s, j], recv.at[s, j], twin)

    def order(swap, j, k):
        return 1 - k if swap and j == 1 else k

    def ring_pass(buf, send, recv, s, k, swap):
        for j in range(2):
            q = order(swap, j, k)
            ring_wait(buf, send, recv, s, j, q)
            if q == j:
                ring_copy(buf, send, recv, s, j, q).start()
            else:
                @pl.when(s < mid - 1)
                def _():
                    ring_copy(buf, send, recv, s, j, q).start()

    def ring_begin(buf, send, recv, k, swap):
        for j in range(2):
            ring_copy(buf, send, recv, 0, j, order(swap, j, k)).start()

    def ring_end(buf, send, recv):
        for j in range(2):
            ring_wait(buf, send, recv, mid, j, j)

    def ring_sent(buf, send, recv):
        for s in range(mid):
            for j in range(2):
                for q in range(2):
                    if s < mid - 1 or q == j:
                        ring_copy(buf, send, recv, s, j, q).wait_send()

    def sides(s):
        return (0,) if isinstance(s, int) and s in (0, mid) else (0, 1)

    def value_copy(buf, send, recv, s, i):
        t = lax.rem(v + i, nv)
        return remote(
            buf.at[s, v], buf.at[s, v], send.at[s, i], recv.at[s, i], at(x, z, lax.rem(t, 2), t // 2)
        )

    def value_wait(buf, send, recv, s, i):
        view = buf.at[s, lax.rem(v - i + nv, nv)]
        remote(view, view, send.at[s, i], recv.at[s, i], twin).wait_recv()

    def live_at(c, i):
        return lax.broadcasted_iota(jnp.int32, (STRIDE, PAD), 0) == offs[c, pl.ds(i, 1), :].astype(jnp.int32)

    def partial_values(buf, send, recv, weight, chunks, s):
        for j in sides(s):
            c = chunk_of(s, j)
            dense = nt(weight[...], chunks[c])
            for i in range(BLK):
                buf[s, v, j * BLK + i : j * BLK + i + 1, :] = jnp.sum(
                    jnp.where(live_at(c, i), dense[i * STRIDE : (i + 1) * STRIDE], 0.0), axis=0, keepdims=True
                )
        for i in range(1, nv):
            value_copy(buf, send, recv, s, i).start()

    def whole_values(buf, send, recv, s):
        for i in range(1, nv):
            value_wait(buf, send, recv, s, i)
        total = buf[s, 0]
        for k in range(1, nv):
            total += buf[s, k]
        return total

    def spread(values, c, i):
        return jnp.where(live_at(c, i), values, 0.0).astype(BF16)

    for q in range(2):
        for i in range(1, nb):
            x_copy(i, q).wait_recv()
        rh[z, :, q * piece : (q + 1) * piece] = nn(pm[...], xbuf[:, q * piece : (q + 1) * piece]).astype(BF16)
        ring_begin(rh, a_send, a_recv, q, False)

    def ro_copy(s, j):
        return twin_copy(rh, ro, d_send, d_recv, s, j)

    def eo_copy(s, j):
        return twin_copy(eh, eo, f_send, f_recv, s, j)

    def encode(s):
        for j in sides(s):
            ro_copy(s, j).start()
        partial_values(va, va_send, va_recv, enct, rh, s)

    def decode(s):
        values = whole_values(va, va_send, va_recv, s)
        vact[s] = values
        chunks = [chunk_of(s, j) for j in sides(s)]
        table = jnp.concatenate([values] + [offs[c] for c in chunks], axis=0).astype(BF16)
        columns = nt(eye[0:SLOTS, :], table)
        place = lax.broadcasted_iota(jnp.int32, (SLOTS, STRIDE), 1).astype(F32)
        total = None
        for i in range(BLK):
            acts = [
                jnp.where(place == columns[:, 8 + 8 * j + i : 9 + 8 * j + i], columns[:, BLK * j + i : BLK * j + i + 1], 0.0)
                for j in range(len(chunks))
            ]
            act = acts[0] if len(acts) == 1 else jnp.concatenate(acts, axis=0)
            term = nn(act.astype(BF16), dech[i * STRIDE : (i + 1) * STRIDE, :])
            total = term if total is None else total + term
        for j, c in enumerate(chunks):
            part[c] = total[j * SLOTS : (j + 1) * SLOTS]

    for c in weights:
        c.wait_recv()
    turn_encoder(1 - h)
    own[1].wait()
    encode(0)
    def encode_step(s, carry):
        ring_pass(rh, a_send, a_recv, s, 0, False)

        @pl.when(s == 2)
        def _():
            decode(0)

        @pl.when(s > 2)
        def _():
            decode(s - 2)

        ring_pass(rh, a_send, a_recv, s, 1, False)

        @pl.when(s == 1)
        def _():
            for i in range(1, Z):
                meta_copy(i).wait_recv()

        encode(s)
        return carry

    lax.fori_loop(1, mid, encode_step, 0)
    decode(mid - 2)
    ring_end(rh, a_send, a_recv)
    encode(mid)
    decode(mid - 1)

    def sum_copy(t, j, q):
        view = pl.ds(q * piece, piece)
        to = at(x, lax.rem(z + (1 - 2 * j) + Z, Z), h, y)
        return remote(
            sbuf.at[j, t - 1, :, view], rbuf.at[j, t - 1, :, view], s_send.at[j, t - 1, q], s_recv.at[j, t - 1, q], to
        )

    def transpose_rows(s):
        for j in sides(s):
            c = chunk_of(s, j)
            ro_copy(s, j).wait_recv()
            for k, src in ((h, rh), (1 - h, ro)):
                for i in range(half // 256):
                    rowst[c, pl.ds(pl.multiple_of(k * half + i * 256, 256), 256), :] = nt(
                        eye[...], src[c, :, i * 256 : (i + 1) * 256]
                    ).astype(BF16)

    def sum_step(t, k):
        for j in range(2):
            q = order(True, j, k)
            low = q * piece
            c = chunk_of(t, 1 - j)
            total = part[c, :, low : low + piece]
            if t < mid - 1 or (t < mid and q == j):
                sum_copy(t + 1, j, q).wait_recv()
                total += rbuf[j, t, :, low : low + piece].astype(F32)
            sbuf[j, t - 1, :, low : low + piece] = total.astype(BF16)
            sum_copy(t, j, q).start()

    sum_step(mid - 1, 1)
    decode(mid)
    sum_step(mid, 0)
    sum_step(mid - 1, 0)
    pmt[...] = nt(eye[0:nr, 0:nr], pm[...]).astype(BF16)
    transpose_rows(0)
    for t in range(mid - 2, 0, -1):
        sum_step(t, 1)
        transpose_rows(t)
        sum_step(t, 0)
    transpose_rows(mid - 1)
    transpose_rows(mid)

    def ret_copy(i, q):
        t = lax.rem(b + i, nb)
        return remote(
            xsend.at[block(t), pl.ds(q * piece, piece)], xret.at[x, :, part_lanes(h, q)],
            r_send.at[i, q], r_recv.at[i, q], at(t // 2, z, lax.rem(t, 2), y),
        )

    def ret_wait(i, q):
        t = lax.rem(b - i + nb, nb)
        view = xret.at[t // 2, :, part_lanes(lax.rem(t, 2), q)]
        remote(view, view, r_send.at[i, q], r_recv.at[i, q], twin).wait_recv()

    def err_copy(i, q):
        t = lax.rem(b + i, nb)
        return remote(
            err_ref.at[:, part_lanes(lax.rem(t, 2), q)], xerr.at[block(b), pl.ds(q * piece, piece)],
            e_send.at[i, q], e_recv.at[i, q], at(t // 2, z, lax.rem(t, 2), y),
        )

    for q in range(2):
        own_lanes = slice(q * piece, (q + 1) * piece)
        for j in range(2):
            sum_copy(1, j, q).wait_recv()
        fin[0:SLOTS, own_lanes] = (
            part[z, :, own_lanes] + rbuf[0, 0, :, own_lanes].astype(F32) + rbuf[1, 0, :, own_lanes].astype(F32)
        ).astype(BF16)
        xsend[:, own_lanes] = nn(pmt[...], fin[:, own_lanes]).astype(BF16)
        for i in range(1, nb):
            ret_copy(i, q).start()
        xret[x, :, part_lanes(h, q)] = xsend[block(b), own_lanes]

    for q in range(2):
        for i in range(1, nb):
            ret_wait(i, q)
        for k in range(2):
            cols = slice(k * half + q * piece, k * half + (q + 1) * piece)
            recon = xret[0, :, cols].astype(F32)
            for e in range(1, X):
                recon += xret[e, :, cols].astype(F32)
            err_ref[:, cols] = (recon - rows_ref[:, cols].astype(F32)).astype(BF16)
        for i in range(1, nb):
            err_copy(i, q).start()
        xerr[block(b), q * piece : (q + 1) * piece] = err_ref[:, part_lanes(h, q)]

    for q in range(2):
        for i in range(1, nb):
            err_copy(i, q).wait_recv()
        eh[z, :, q * piece : (q + 1) * piece] = nn(pm[...], xerr[:, q * piece : (q + 1) * piece]).astype(BF16)
        ring_begin(eh, b_send, b_recv, q, False)

    def latent_grads(s):
        for j in sides(s):
            eo_copy(s, j).start()
        partial_values(vg, vg_send, vg_recv, dech, eh, s)

    def add_dec(s):
        for j in sides(s):
            eo_copy(s, j).wait_recv()
        nblk = lat // STRIDE
        acts = []
        for j in sides(s):
            c = chunk_of(s, j)
            blocks = [spread(vact[s, pl.ds(j * BLK + h * nblk + i, 1), :], c, h * nblk + i) for i in range(nblk)]
            acts.append((c, jnp.concatenate(blocks, axis=0)))
        for k, src in ((h, eh), (1 - h, eo)):
            gdec_ref[:, lanes(k)] += sum(nn(a, src[c]) for c, a in acts)

    def add_enc(s):
        vpre[s] = whole_values(vg, vg_send, vg_recv, s)
        for i in range(lat // STRIDE):
            blk = h * (lat // STRIDE) + i
            low = i * STRIDE
            pres = [(chunk_of(s, j), spread(vpre[s, pl.ds(j * BLK + blk, 1), :], chunk_of(s, j), blk)) for j in sides(s)]
            for k in range(2):
                cols = slice(k * half, (k + 1) * half)
                genc_ref[cols, low : low + STRIDE] += sum(nt(rowst[c, cols, :], g) for c, g in pres)

    latent_grads(0)

    def gradient_step(s, carry):
        ring_pass(eh, b_send, b_recv, s, 0, False)

        @pl.when(s == 1)
        def _():
            add_dec(0)

        @pl.when(s == 2)
        def _():
            add_enc(0)

        @pl.when(s > 2)
        def _():
            add_enc(s - 2)

        ring_pass(eh, b_send, b_recv, s, 1, False)
        latent_grads(s)

        @pl.when(s > 1)
        def _():
            add_dec(s - 1)

        return carry

    lax.fori_loop(1, mid, gradient_step, 0)
    add_enc(mid - 2)
    ring_end(eh, b_send, b_recv)
    latent_grads(mid)
    add_dec(mid - 1)
    add_enc(mid - 1)
    add_dec(mid)
    add_enc(mid)

    for i in range(1, nb):
        route_copy(i).wait_send()
        for q in range(2):
            x_copy(i, q).wait_send()
            ret_copy(i, q).wait_send()
            err_copy(i, q).wait_send()
    for c in weights:
        c.wait_send()
    for i in range(1, Z):
        meta_copy(i).wait_send()
    ring_sent(rh, a_send, a_recv)
    ring_sent(eh, b_send, b_recv)
    for t in range(mid, 0, -1):
        for j in range(2):
            for q in range(2):
                if t < mid or q == j:
                    sum_copy(t, j, q).wait_send()

    def sent(s):
        for i in range(1, nv):
            value_copy(va, va_send, va_recv, s, i).wait_send()
            value_copy(vg, vg_send, vg_recv, s, i).wait_send()
        for j in sides(s):
            ro_copy(s, j).wait_send()
            eo_copy(s, j).wait_send()

    def sent_step(s, carry):
        sent(s)
        return carry

    sent(0)
    lax.fori_loop(1, mid, sent_step, 0)
    sent(mid)


def per_device(experts, topk, cap, rows_in, expert_picks, latent_ids, enc_weight, dec_weight):
    X, Y = experts, lax.axis_size("chan")
    Z = lax.axis_size("expert") // (2 * X)
    rd, width = rows_in.shape
    lat, half, mid = enc_weight.shape[1], width // 2, Z // 2
    nb, nv = 2 * X, 2 * Y
    slots = min(-(-cap * nb // 16) * 16, PAD)
    vmem, hbm = pl.BlockSpec(memory_space=pltpu.VMEM), pl.BlockSpec(memory_space=pltpu.HBM)
    dma = pltpu.SemaphoreType.DMA
    scratch = [
        pltpu.VMEM(rows_in.shape, BF16),
        pltpu.VMEM((2, rd), jnp.int32),
        pltpu.VMEM(latent_ids.shape, jnp.int32),
        pltpu.VMEM((rd, META), BF16),
        pltpu.VMEM((nb * rd, META), BF16),
        pltpu.VMEM((nb * rd, half), BF16),
        pltpu.VMEM((Z, PAD, half), BF16),
        pltpu.VMEM((Z, PAD, half), BF16),
        pltpu.VMEM((Z, PAD, half), BF16),
        pltpu.VMEM((Z, PAD, half), BF16),
        pltpu.VMEM((Z, width, PAD), BF16),
        pltpu.VMEM((2, half, lat), BF16),
        pltpu.VMEM((2 * lat, half), BF16),
        pltpu.VMEM((2 * lat, half), BF16),
        pltpu.VMEM((PAD, PAD), BF16),
        pltpu.VMEM((PAD, nb * rd), BF16),
        pltpu.VMEM((nb * rd, PAD), BF16),
        pltpu.VMEM((Z, 8, PAD), F32),
        pltpu.VMEM((Z, 8, PAD), F32),
        pltpu.VMEM((mid + 1, nv, 8, PAD), F32),
        pltpu.VMEM((mid + 1, nv, 8, PAD), F32),
        pltpu.VMEM((mid + 1, 8, PAD), F32),
        pltpu.VMEM((mid + 1, 8, PAD), F32),
        pltpu.VMEM((Z, slots, half), F32),
        pltpu.VMEM((2, mid, slots, half), BF16),
        pltpu.VMEM((2, mid, slots, half), BF16),
        pltpu.VMEM((PAD, half), BF16),
        pltpu.VMEM((nb * rd, half), BF16),
        pltpu.VMEM((X, rd, width), BF16),
        pltpu.VMEM((nb * rd, half), BF16),
        dma((6,)),
    ]
    pairs = [(nb,), (2,), (nb, 2), (Z,), (mid + 1, nv), (mid + 1, nv), (2, mid, 2), (2, mid, 2), (2, mid, 2)]
    pairs += [(nb, 2), (nb, 2), (mid + 1, 2), (mid + 1, 2)]
    for shape in pairs:
        scratch += [dma(shape), dma(shape)]
    operands = (rows_in, expert_picks.T, latent_ids, enc_weight, dec_weight)
    return pl.pallas_call(
        functools.partial(step_kernel, X, Y, Z, slots, topk),
        out_shape=(
            pltpu.VMEM(rows_in.shape, BF16),
            pltpu.VMEM(enc_weight.shape, F32),
            pltpu.VMEM(dec_weight.shape, F32),
        ),
        in_specs=[hbm] * 5,
        out_specs=(vmem, vmem, vmem),
        scratch_shapes=scratch,
        compiler_params=pltpu.CompilerParams(
            collective_id=0, has_side_effects=True, vmem_limit_bytes=46 * 2**20
        ),
    )(*(pltpu.with_memory_space_constraint(a, pltpu.HBM) for a in operands))


def solution(mesh, experts=EXPERTS, topk=TOPK, cap=CAP):
    placed = (
        P("expert", "chan"),
        P("expert", None),
        P("expert", None, None),
        P("chan", "expert"),
        P("expert", "chan"),
    )
    return jax.shard_map(
        functools.partial(per_device, experts, topk, cap),
        mesh=mesh,
        in_specs=placed,
        out_specs=(P("expert", "chan"), P("chan", "expert"), P("expert", "chan")),
        check_vma=False,
    )
```

```python
import functools

import jax
import jax.numpy as jnp
from jax import lax
from jax.experimental import pallas as pl
from jax.experimental.pallas import tpu as pltpu
from jax.sharding import PartitionSpec as P

EXPERTS = 4
TOPK = 32
CAP = 18

STRIDE = 256
BLK = 4
META = 128
PAD = 256
MESH = pl.DeviceIdType.MESH
F32, BF16 = jnp.float32, jnp.bfloat16


def nt(a, b):
    return lax.dot_general(a, b, (((1,), (1,)), ((), ())), preferred_element_type=F32)


def nn(a, b):
    return jnp.dot(a, b, preferred_element_type=F32)


def step_kernel(
    X, Y, Z, SLOTS, TOPK,
    rows_hbm, picks_hbm, ids_hbm, enc_ref, dec_ref,
    err_ref, genc_ref, gdec_ref,
    rows_ref, picks_ref, ids_ref, meta_ref, xmeta, xbuf, rh, ro, eh, eo, rowst, est, enct, dech, eye, pm, pmt, offs_out, offs,
    va, vg, vact, vpre, part, sbuf, rbuf, fin, xsend, xret, xerr,
    local_sem, q_send, q_recv, w_send, w_recv, x_send, x_recv, m_send, m_recv, va_send, va_recv,
    vg_send, vg_recv, a_send, a_recv, b_send, b_recv, s_send, s_recv,
    r_send, r_recv, e_send, e_recv, d_send, d_recv, f_send, f_recv,
):
    p, y = lax.axis_index("expert"), lax.axis_index("chan")
    h, z, x = lax.rem(p, 2), lax.rem(p // 2, Z), p // (2 * Z)
    b, v = x * 2 + h, y * 2 + h
    nb, nv = 2 * X, 2 * Y
    rd, width = rows_ref.shape
    half, lat = width // 2, enc_ref.shape[1]
    piece, mid = half // 2, Z // 2

    def at(x_, z_, h_, y_):
        return ((x_ * Z + z_) * 2 + h_, y_)

    twin = at(x, z, 1 - h, y)

    def remote(src, dst, send, recv, to):
        return pltpu.make_async_remote_copy(
            src_ref=src, dst_ref=dst, send_sem=send, recv_sem=recv, device_id=to, device_id_type=MESH
        )

    def lanes(k):
        return pl.ds(pl.multiple_of(k * half, 128), half)

    def block(k):
        return pl.ds(pl.multiple_of(k * rd, rd), rd)

    def chunk_of(s, j):
        return lax.rem(z + (2 * j - 1) * s + Z, Z)

    small_in = [
        pltpu.make_async_copy(src, dst, local_sem.at[3 + n])
        for n, (src, dst) in enumerate(((rows_hbm, rows_ref), (picks_hbm, picks_ref), (ids_hbm, ids_ref)))
    ]
    for c in small_in:
        c.start()

    barrier = pltpu.get_barrier_semaphore()
    for i in range(1, nb):
        t = lax.rem(b + i, nb)
        pl.semaphore_signal(barrier, inc=1, device_id=at(t // 2, z, lax.rem(t, 2), y), device_id_type=MESH)
    for i in range(1, Z):
        pl.semaphore_signal(barrier, inc=1, device_id=at(x, lax.rem(z + i, Z), h, y), device_id_type=MESH)
    for i in range(1, Y):
        for k in range(2):
            pl.semaphore_signal(barrier, inc=1, device_id=at(x, z, k, lax.rem(y + i, Y)), device_id_type=MESH)
    down = lax.broadcasted_iota(jnp.int32, (PAD, PAD), 0)
    across = lax.broadcasted_iota(jnp.int32, (PAD, PAD), 1)
    eye[...] = jnp.where(down == across, 1.0, 0.0).astype(BF16)
    for buf in (rh, ro, eh, eo):
        buf[:, SLOTS:, :] = jnp.zeros((Z, PAD - SLOTS, half), BF16)
    fin[SLOTS:, :] = jnp.zeros((PAD - SLOTS, half), BF16)
    for s in range(mid + 1):
        va[v, s] = jnp.zeros((8, PAD), F32)
        vg[v, s] = jnp.zeros((8, PAD), F32)
    genc_ref[...] = jnp.zeros_like(genc_ref)
    gdec_ref[...] = jnp.zeros_like(gdec_ref)

    for c in small_in:
        c.wait()
    starts = lax.broadcasted_iota(jnp.int32, (rd, TOPK), 1) * STRIDE
    first = lax.broadcasted_iota(jnp.int32, (16, rd), 0) == 0
    picked = jnp.where(first, picks_ref[0:1, :], picks_ref[1:2, :]).astype(F32).astype(BF16)
    small = lax.broadcasted_iota(jnp.int32, (rd, rd), 0) == lax.broadcasted_iota(jnp.int32, (rd, rd), 1)
    pick_columns = nt(jnp.where(small, 1.0, 0.0).astype(BF16), picked)
    meta_ref[...] = jnp.concatenate(
        [(ids_ref[:, k, :] - starts).astype(F32) for k in range(2)]
        + [pick_columns, jnp.zeros((rd, META - 2 * TOPK - 16), F32)],
        axis=1,
    ).astype(BF16)
    xmeta[block(b), :] = meta_ref[...]
    xbuf[block(b), :] = rows_ref[:, lanes(h)]
    pl.semaphore_wait(barrier, nb - 1 + Z - 1 + 2 * (Y - 1))

    def part_lanes(k, q):
        return pl.ds(pl.multiple_of(k * half + q * piece, 128), piece)

    def near(i):
        t = lax.rem(b + i, nb)
        return lax.rem(t, 2), at(t // 2, z, lax.rem(t, 2), y)

    def route_copy(i):
        _, to = near(i)
        return remote(meta_ref, xmeta.at[block(b)], q_send.at[i], q_recv.at[i], to)

    def x_copy(i, q):
        k, to = near(i)
        return remote(
            rows_ref.at[:, part_lanes(k, q)], xbuf.at[block(b), pl.ds(q * piece, piece)],
            x_send.at[i, q], x_recv.at[i, q], to,
        )

    mine = pl.ds(pl.multiple_of(h * lat, lat), lat)
    own = [
        pltpu.make_async_copy(enc_ref.at[lanes(h), :], est.at[h], local_sem.at[0]),
        pltpu.make_async_copy(dec_ref.at[:, lanes(h)], dech.at[mine], local_sem.at[1]),
    ]
    weights = [
        remote(enc_ref.at[lanes(1 - h), :], est.at[h], w_send.at[0], w_recv.at[0], twin),
        remote(dec_ref.at[:, lanes(1 - h)], dech.at[mine], w_send.at[1], w_recv.at[1], twin),
    ]
    for i in range(1, nb):
        route_copy(i).start()
    for q in range(2):
        for i in range(1, nb):
            x_copy(i, q).start()
    for c in own + weights:
        c.start()

    def turn_encoder(k):
        for i in range(lat // STRIDE):
            low = pl.multiple_of(k * lat + i * STRIDE, STRIDE)
            enct[pl.ds(low, STRIDE), :] = nt(
                eye[...], est[k, :, i * STRIDE : (i + 1) * STRIDE]
            ).astype(BF16)

    for i in range(1, nb):
        route_copy(i).wait_recv()
    nr = xbuf.shape[0]
    meta_t = nt(eye[0:META, 0:META], xmeta[...])
    xf = x.astype(F32)
    hit0 = meta_t[2 * TOPK : 2 * TOPK + 1] == xf
    hit1 = meta_t[2 * TOPK + 1 : 2 * TOPK + 2] == xf
    hit = jnp.where(hit0, 1.0, jnp.where(hit1, 1.0, 0.0))
    offe = jnp.where(hit0, meta_t[0:TOPK], jnp.where(hit1, meta_t[TOPK : 2 * TOPK], 0.0)).astype(BF16)
    before = jnp.where(down[0:nr, 0:nr] < across[0:nr, 0:nr], 1.0, 0.0).astype(BF16)
    rank = nn(jnp.broadcast_to(hit, (16, nr)).astype(BF16), before)[0:1]
    slot = jnp.where(hit > 0.5, rank, -1.0).astype(jnp.int32)
    pm[...] = jnp.where(down[:, 0:nr] == slot, 1.0, 0.0).astype(BF16)
    offs_t = nt(offe, pm[...])
    for k in range(Z):
        mine = offs_t[k * BLK : (k + 1) * BLK]
        offs_out[k] = jnp.concatenate([mine, mine], axis=0)

    def meta_copy(i):
        t = lax.rem(z + i, Z)
        return remote(offs_out.at[t], offs.at[z], m_send.at[i], m_recv.at[i], at(x, t, h, y))

    for i in range(1, Z):
        meta_copy(i).start()
    offs[z] = offs_out[z]
    own[0].wait()
    turn_encoder(h)

    def ring_copy(buf, send, recv, s, j, q):
        c = chunk_of(s, j)
        view = buf.at[c, pl.ds(0, SLOTS), pl.ds(q * piece, piece)]
        to = at(x, lax.rem(z + (1 - 2 * j) + Z, Z), h, y)
        return remote(view, view, send.at[j, s, q], recv.at[j, s, q], to)

    def ring_wait(buf, send, recv, s, j, q):
        c = chunk_of(s, j)
        view = buf.at[c, pl.ds(0, SLOTS), pl.ds(q * piece, piece)]
        remote(view, view, send.at[j, s - 1, q], recv.at[j, s - 1, q], twin).wait_recv()

    def twin_copy(src, dst, send, recv, s, j):
        c = chunk_of(s, j)
        return remote(src.at[c, pl.ds(0, SLOTS)], dst.at[c, pl.ds(0, SLOTS)], send.at[s, j], recv.at[s, j], twin)

    def order(swap, j, k):
        return 1 - k if swap and j == 1 else k

    def ring_pass(buf, send, recv, s, k, swap):
        for j in range(2):
            q = order(swap, j, k)
            ring_wait(buf, send, recv, s, j, q)
            if q == j:
                ring_copy(buf, send, recv, s, j, q).start()
            else:
                @pl.when(s < mid - 1)
                def _():
                    ring_copy(buf, send, recv, s, j, q).start()

    def ring_begin(buf, send, recv, k, swap):
        for j in range(2):
            ring_copy(buf, send, recv, 0, j, order(swap, j, k)).start()

    def ring_end(buf, send, recv):
        for j in range(2):
            ring_wait(buf, send, recv, mid, j, j)

    def ring_sent(buf, send, recv):
        for s in range(mid):
            for j in range(2):
                for q in range(2):
                    if s < mid - 1 or q == j:
                        ring_copy(buf, send, recv, s, j, q).wait_send()

    def sides(s):
        return (0,) if isinstance(s, int) and s in (0, mid) else (0, 1)

    def run_of(buf, g):
        if buf is va:
            return (pl.ds(0, mid), pl.ds(mid, 1))[g]
        return pl.ds(2 * g, 1 if isinstance(g, int) and 2 * g == mid else 2)

    def value_copy(buf, send, recv, g, i):
        t = lax.rem(v + i, nv)
        view = buf.at[v, run_of(buf, g)]
        return remote(view, view, send.at[g, i], recv.at[g, i], at(x, z, lax.rem(t, 2), t // 2))

    def values_start(buf, send, recv, g):
        for i in range(1, nv):
            value_copy(buf, send, recv, g, i).start()

    def values_wait(buf, send, recv, g):
        for i in range(1, nv):
            view = buf.at[lax.rem(v - i + nv, nv), run_of(buf, g)]
            remote(view, view, send.at[g, i], recv.at[g, i], twin).wait_recv()

    def values_left(buf, send, recv, g):
        for i in range(1, nv):
            value_copy(buf, send, recv, g, i).wait_send()

    def live_at(c, i):
        return lax.broadcasted_iota(jnp.int32, (STRIDE, PAD), 0) == offs[c, pl.ds(i, 1), :].astype(jnp.int32)

    def partial_values(buf, weight, chunks, s):
        for j in sides(s):
            c = chunk_of(s, j)
            dense = nt(weight[...], chunks[c])
            for i in range(BLK):
                buf[v, s, j * BLK + i : j * BLK + i + 1, :] = jnp.sum(
                    jnp.where(live_at(c, i), dense[i * STRIDE : (i + 1) * STRIDE], 0.0), axis=0, keepdims=True
                )

    def whole_values(buf, s):
        total = buf[0, s]
        for k in range(1, nv):
            total += buf[k, s]
        return total

    def spread(values, c, i):
        return jnp.where(live_at(c, i), values, 0.0).astype(BF16)

    for q in range(2):
        for i in range(1, nb):
            x_copy(i, q).wait_recv()
        rh[z, :, q * piece : (q + 1) * piece] = nn(pm[...], xbuf[:, q * piece : (q + 1) * piece]).astype(BF16)
        ring_begin(rh, a_send, a_recv, q, False)

    def ro_copy():
        return remote(rh.at[:, pl.ds(0, SLOTS)], ro.at[:, pl.ds(0, SLOTS)], d_send.at[0], d_recv.at[0], twin)

    def eo_copy(s, j):
        return twin_copy(eh, eo, f_send, f_recv, s, j)

    def encode(s):
        partial_values(va, enct, rh, s)

    def decode(s):
        values = whole_values(va, s)
        vact[s] = values
        chunks = [chunk_of(s, j) for j in sides(s)]
        table = jnp.concatenate([values] + [offs[c] for c in chunks], axis=0).astype(BF16)
        columns = nt(eye[0:SLOTS, :], table)
        place = lax.broadcasted_iota(jnp.int32, (SLOTS, STRIDE), 1).astype(F32)
        total = None
        for i in range(BLK):
            acts = [
                jnp.where(place == columns[:, 8 + 8 * j + i : 9 + 8 * j + i], columns[:, BLK * j + i : BLK * j + i + 1], 0.0)
                for j in range(len(chunks))
            ]
            act = acts[0] if len(acts) == 1 else jnp.concatenate(acts, axis=0)
            term = nn(act.astype(BF16), dech[i * STRIDE : (i + 1) * STRIDE, :])
            total = term if total is None else total + term
        for j, c in enumerate(chunks):
            part[c] = total[j * SLOTS : (j + 1) * SLOTS]

    for c in weights:
        c.wait_recv()
    turn_encoder(1 - h)
    own[1].wait()
    encode(0)
    def encode_step(s, carry):
        ring_pass(rh, a_send, a_recv, s, 0, False)
        ring_pass(rh, a_send, a_recv, s, 1, False)

        @pl.when(s == 1)
        def _():
            for i in range(1, Z):
                meta_copy(i).wait_recv()

        encode(s)
        return carry

    lax.fori_loop(1, mid, encode_step, 0)
    values_start(va, va_send, va_recv, 0)
    ring_end(rh, a_send, a_recv)
    encode(mid)
    values_start(va, va_send, va_recv, 1)
    ro_copy().start()
    values_wait(va, va_send, va_recv, 0)
    decode(mid - 1)

    def sum_copy(t, j, q):
        view = pl.ds(q * piece, piece)
        to = at(x, lax.rem(z + (1 - 2 * j) + Z, Z), h, y)
        return remote(
            sbuf.at[j, t - 1, :, view], rbuf.at[j, t - 1, :, view], s_send.at[j, t - 1, q], s_recv.at[j, t - 1, q], to
        )

    def transpose_rows(k, src, s):
        for j in sides(s):
            c = chunk_of(s, j)
            for i in range(half // 256):
                rowst[c, pl.ds(pl.multiple_of(k * half + i * 256, 256), 256), :] = nt(
                    eye[...], src[c, :, i * 256 : (i + 1) * 256]
                ).astype(BF16)

    def sum_step(t, k):
        for j in range(2):
            q = order(True, j, k)
            low = q * piece
            c = chunk_of(t, 1 - j)
            total = part[c, :, low : low + piece]
            if t < mid - 1 or (t < mid and q == j):
                sum_copy(t + 1, j, q).wait_recv()
                total += rbuf[j, t, :, low : low + piece].astype(F32)
            sbuf[j, t - 1, :, low : low + piece] = total.astype(BF16)
            sum_copy(t, j, q).start()

    sum_step(mid - 1, 1)
    decode(mid - 2)
    values_wait(va, va_send, va_recv, 1)
    decode(mid)
    sum_step(mid, 0)
    transpose_rows(h, rh, mid)
    sum_step(mid - 1, 0)
    pmt[...] = nt(eye[0:nr, 0:nr], pm[...]).astype(BF16)
    transpose_rows(h, rh, 0)
    for t in range(mid - 2, 0, -1):
        sum_step(t, 1)
        decode(t - 1)
        transpose_rows(h, rh, t)
        sum_step(t, 0)
    transpose_rows(h, rh, mid - 1)
    ro_copy().wait_recv()
    for s in range(mid + 1):
        transpose_rows(1 - h, ro, s)

    def ret_copy(i, q):
        t = lax.rem(b + i, nb)
        return remote(
            xsend.at[block(t), pl.ds(q * piece, piece)], xret.at[x, :, part_lanes(h, q)],
            r_send.at[i, q], r_recv.at[i, q], at(t // 2, z, lax.rem(t, 2), y),
        )

    def ret_wait(i, q):
        t = lax.rem(b - i + nb, nb)
        view = xret.at[t // 2, :, part_lanes(lax.rem(t, 2), q)]
        remote(view, view, r_send.at[i, q], r_recv.at[i, q], twin).wait_recv()

    def err_copy(i, q):
        t = lax.rem(b + i, nb)
        return remote(
            err_ref.at[:, part_lanes(lax.rem(t, 2), q)], xerr.at[block(b), pl.ds(q * piece, piece)],
            e_send.at[i, q], e_recv.at[i, q], at(t // 2, z, lax.rem(t, 2), y),
        )

    for q in range(2):
        own_lanes = slice(q * piece, (q + 1) * piece)
        for j in range(2):
            sum_copy(1, j, q).wait_recv()
        fin[0:SLOTS, own_lanes] = (
            part[z, :, own_lanes] + rbuf[0, 0, :, own_lanes].astype(F32) + rbuf[1, 0, :, own_lanes].astype(F32)
        ).astype(BF16)
        xsend[:, own_lanes] = nn(pmt[...], fin[:, own_lanes]).astype(BF16)
        for i in range(1, nb):
            ret_copy(i, q).start()
        xret[x, :, part_lanes(h, q)] = xsend[block(b), own_lanes]

    for q in range(2):
        for i in range(1, nb):
            ret_wait(i, q)
        for k in range(2):
            cols = slice(k * half + q * piece, k * half + (q + 1) * piece)
            recon = xret[0, :, cols].astype(F32)
            for e in range(1, X):
                recon += xret[e, :, cols].astype(F32)
            err_ref[:, cols] = (recon - rows_ref[:, cols].astype(F32)).astype(BF16)
        for i in range(1, nb):
            err_copy(i, q).start()
        xerr[block(b), q * piece : (q + 1) * piece] = err_ref[:, part_lanes(h, q)]

    for q in range(2):
        for i in range(1, nb):
            err_copy(i, q).wait_recv()
        eh[z, :, q * piece : (q + 1) * piece] = nn(pm[...], xerr[:, q * piece : (q + 1) * piece]).astype(BF16)
        ring_begin(eh, b_send, b_recv, q, False)

    def latent_grads(s):
        for j in sides(s):
            eo_copy(s, j).start()
        partial_values(vg, dech, eh, s)

    def add_dec(s):
        for j in sides(s):
            eo_copy(s, j).wait_recv()
        nblk = lat // STRIDE
        acts = []
        for j in sides(s):
            c = chunk_of(s, j)
            blocks = [spread(vact[s, pl.ds(j * BLK + h * nblk + i, 1), :], c, h * nblk + i) for i in range(nblk)]
            acts.append((c, jnp.concatenate(blocks, axis=0)))
        for k, src in ((h, eh), (1 - h, eo)):
            gdec_ref[:, lanes(k)] += sum(nn(a, src[c]) for c, a in acts)

    def add_enc(s):
        vpre[s] = whole_values(vg, s)
        for i in range(lat // STRIDE):
            blk = h * (lat // STRIDE) + i
            low = i * STRIDE
            pres = [(chunk_of(s, j), spread(vpre[s, pl.ds(j * BLK + blk, 1), :], chunk_of(s, j), blk)) for j in sides(s)]
            for k in range(2):
                cols = slice(k * half, (k + 1) * half)
                genc_ref[cols, low : low + STRIDE] += sum(nt(rowst[c, cols, :], g) for c, g in pres)

    latent_grads(0)

    def gradient_step(s, carry):
        ring_pass(eh, b_send, b_recv, s, 0, False)

        @pl.when(s == 1)
        def _():
            add_dec(0)

        @pl.when(s == 2)
        def _():
            values_wait(vg, vg_send, vg_recv, 0)
            add_enc(0)

        @pl.when(s == 3)
        def _():
            add_enc(1)

        ring_pass(eh, b_send, b_recv, s, 1, False)
        latent_grads(s)

        @pl.when(lax.rem(s, 2) == 1)
        def _():
            values_start(vg, vg_send, vg_recv, s // 2)

        @pl.when(s > 1)
        def _():
            add_dec(s - 1)

        return carry

    lax.fori_loop(1, mid, gradient_step, 0)
    ring_end(eh, b_send, b_recv)
    latent_grads(mid)
    values_start(vg, vg_send, vg_recv, mid // 2)
    add_dec(mid - 1)
    values_wait(vg, vg_send, vg_recv, mid // 2 - 1)
    add_enc(mid - 2)
    add_enc(mid - 1)
    add_dec(mid)
    values_wait(vg, vg_send, vg_recv, mid // 2)
    add_enc(mid)

    for i in range(1, nb):
        route_copy(i).wait_send()
        for q in range(2):
            x_copy(i, q).wait_send()
            ret_copy(i, q).wait_send()
            err_copy(i, q).wait_send()
    for c in weights:
        c.wait_send()
    for i in range(1, Z):
        meta_copy(i).wait_send()
    ring_sent(rh, a_send, a_recv)
    ring_sent(eh, b_send, b_recv)
    for t in range(mid, 0, -1):
        for j in range(2):
            for q in range(2):
                if t < mid or q == j:
                    sum_copy(t, j, q).wait_send()

    for g in range(2):
        values_left(va, va_send, va_recv, g)
    for g in range(mid // 2 + 1):
        values_left(vg, vg_send, vg_recv, g)
    ro_copy().wait_send()

    def eo_left(s):
        for j in sides(s):
            eo_copy(s, j).wait_send()

    def eo_left_step(s, carry):
        eo_left(s)
        return carry

    eo_left(0)
    lax.fori_loop(1, mid, eo_left_step, 0)
    eo_left(mid)


def write_out(*refs):
    srcs, dsts, sems = refs[:3], refs[3:6], refs[6]
    copies = []
    for src, dst, parts in zip(srcs, dsts, (1, 4, 4)):
        n = src.shape[0] // parts
        for k in range(parts):
            rows = pl.ds(k * n, n)
            copies.append(pltpu.make_async_copy(src.at[rows], dst.at[rows], sems.at[len(copies)]))
    for c in copies:
        c.start()
    for c in copies:
        c.wait()


def per_device(experts, topk, cap, rows_in, expert_picks, latent_ids, enc_weight, dec_weight):
    X, Y = experts, lax.axis_size("chan")
    Z = lax.axis_size("expert") // (2 * X)
    rd, width = rows_in.shape
    lat, half, mid = enc_weight.shape[1], width // 2, Z // 2
    nb, nv = 2 * X, 2 * Y
    slots = min(-(-cap * nb // 16) * 16, PAD)
    vmem, hbm = pl.BlockSpec(memory_space=pltpu.VMEM), pl.BlockSpec(memory_space=pltpu.HBM)
    dma = pltpu.SemaphoreType.DMA
    scratch = [
        pltpu.VMEM(rows_in.shape, BF16),
        pltpu.VMEM((2, rd), jnp.int32),
        pltpu.VMEM(latent_ids.shape, jnp.int32),
        pltpu.VMEM((rd, META), BF16),
        pltpu.VMEM((nb * rd, META), BF16),
        pltpu.VMEM((nb * rd, half), BF16),
        pltpu.VMEM((Z, PAD, half), BF16),
        pltpu.VMEM((Z, PAD, half), BF16),
        pltpu.VMEM((Z, PAD, half), BF16),
        pltpu.VMEM((Z, PAD, half), BF16),
        pltpu.VMEM((Z, width, PAD), BF16),
        pltpu.VMEM((2, half, lat), BF16),
        pltpu.VMEM((2 * lat, half), BF16),
        pltpu.VMEM((2 * lat, half), BF16),
        pltpu.VMEM((PAD, PAD), BF16),
        pltpu.VMEM((PAD, nb * rd), BF16),
        pltpu.VMEM((nb * rd, PAD), BF16),
        pltpu.VMEM((Z, 8, PAD), F32),
        pltpu.VMEM((Z, 8, PAD), F32),
        pltpu.VMEM((nv, mid + 1, 8, PAD), F32),
        pltpu.VMEM((nv, mid + 1, 8, PAD), F32),
        pltpu.VMEM((mid + 1, 8, PAD), F32),
        pltpu.VMEM((mid + 1, 8, PAD), F32),
        pltpu.VMEM((Z, slots, half), F32),
        pltpu.VMEM((2, mid, slots, half), BF16),
        pltpu.VMEM((2, mid, slots, half), BF16),
        pltpu.VMEM((PAD, half), BF16),
        pltpu.VMEM((nb * rd, half), BF16),
        pltpu.VMEM((X, rd, width), BF16),
        pltpu.VMEM((nb * rd, half), BF16),
        dma((6,)),
    ]
    pairs = [(nb,), (2,), (nb, 2), (Z,), (2, nv), (mid // 2 + 1, nv), (2, mid, 2), (2, mid, 2), (2, mid, 2)]
    pairs += [(nb, 2), (nb, 2), (1,), (mid + 1, 2)]
    for shape in pairs:
        scratch += [dma(shape), dma(shape)]
    operands = (rows_in, expert_picks.T, latent_ids, enc_weight, dec_weight)
    results = pl.pallas_call(
        functools.partial(step_kernel, X, Y, Z, slots, topk),
        out_shape=(
            pltpu.VMEM(rows_in.shape, BF16),
            pltpu.VMEM(enc_weight.shape, F32),
            pltpu.VMEM(dec_weight.shape, F32),
        ),
        in_specs=[hbm] * 5,
        out_specs=(vmem, vmem, vmem),
        scratch_shapes=scratch,
        compiler_params=pltpu.CompilerParams(
            collective_id=0, has_side_effects=True, vmem_limit_bytes=46 * 2**20
        ),
    )(*(pltpu.with_memory_space_constraint(a, pltpu.HBM) for a in operands))
    return pl.pallas_call(
        write_out,
        out_shape=tuple(jax.ShapeDtypeStruct(r.shape, r.dtype) for r in results),
        in_specs=[vmem] * 3,
        out_specs=(hbm,) * 3,
        scratch_shapes=[dma((9,))],
        compiler_params=pltpu.CompilerParams(vmem_limit_bytes=2 * 2**20),
    )(*(pltpu.with_memory_space_constraint(r, pltpu.VMEM) for r in results))


def solution(mesh, experts=EXPERTS, topk=TOPK, cap=CAP):
    placed = (
        P("expert", "chan"),
        P("expert", None),
        P("expert", None, None),
        P("chan", "expert"),
        P("expert", "chan"),
    )
    return jax.shard_map(
        functools.partial(per_device, experts, topk, cap),
        mesh=mesh,
        in_specs=placed,
        out_specs=(P("expert", "chan"), P("chan", "expert"), P("expert", "chan")),
        check_vma=False,
    )
```

```python
import functools

import jax
import jax.numpy as jnp
from jax import lax
from jax.experimental import pallas as pl
from jax.experimental.pallas import tpu as pltpu
from jax.sharding import PartitionSpec as P

EXPERTS = 4
TOPK = 32
CAP = 18

STRIDE = 256
BLK = 4
META = 128
PAD = 256
MESH = pl.DeviceIdType.MESH
F32, BF16 = jnp.float32, jnp.bfloat16


def nt(a, b):
    return lax.dot_general(a, b, (((1,), (1,)), ((), ())), preferred_element_type=F32)


def nn(a, b):
    return jnp.dot(a, b, preferred_element_type=F32)


def step_kernel(
    X, Y, Z, SLOTS, TOPK,
    rows_hbm, picks_hbm, ids_hbm, enc_ref, dec_ref,
    err_ref, genc_ref, gdec_ref,
    rows_ref, picks_ref, ids_ref, meta_ref, xmeta, xbuf, rh, ro, eh, eo, rowst, est, enct, dech, eye, pm, pmt, offs_out, offs,
    va, vg, vact, vpre, part, sbuf, rbuf, fin, xsend, xret, xerr,
    local_sem, q_send, q_recv, w_send, w_recv, x_send, x_recv, m_send, m_recv, va_send, va_recv,
    vg_send, vg_recv, a_send, a_recv, b_send, b_recv, s_send, s_recv,
    r_send, r_recv, e_send, e_recv, d_send, d_recv, f_send, f_recv,
):
    p, y = lax.axis_index("expert"), lax.axis_index("chan")
    h, z, x = lax.rem(p, 2), lax.rem(p // 2, Z), p // (2 * Z)
    b, v = x * 2 + h, y * 2 + h
    nb, nv = 2 * X, 2 * Y
    rd, width = rows_ref.shape
    half, lat = width // 2, enc_ref.shape[1]
    piece, mid = half // 2, Z // 2

    def at(x_, z_, h_, y_):
        return ((x_ * Z + z_) * 2 + h_, y_)

    twin = at(x, z, 1 - h, y)

    def remote(src, dst, send, recv, to):
        return pltpu.make_async_remote_copy(
            src_ref=src, dst_ref=dst, send_sem=send, recv_sem=recv, device_id=to, device_id_type=MESH
        )

    def lanes(k):
        return pl.ds(pl.multiple_of(k * half, 128), half)

    def block(k):
        return pl.ds(pl.multiple_of(k * rd, rd), rd)

    def chunk_of(s, j):
        return lax.rem(z + (2 * j - 1) * s + Z, Z)

    small_in = [
        pltpu.make_async_copy(src, dst, local_sem.at[3 + n])
        for n, (src, dst) in enumerate(((rows_hbm, rows_ref), (picks_hbm, picks_ref), (ids_hbm, ids_ref)))
    ]
    mine = pl.ds(pl.multiple_of(h * lat, lat), lat)
    own = [
        pltpu.make_async_copy(enc_ref.at[lanes(h), :], est.at[h], local_sem.at[0]),
        pltpu.make_async_copy(dec_ref.at[:, lanes(h)], dech.at[mine], local_sem.at[1]),
    ]
    for c in small_in + own:
        c.start()

    barrier = pltpu.get_barrier_semaphore()
    for i in range(1, nb):
        t = lax.rem(b + i, nb)
        pl.semaphore_signal(barrier, inc=1, device_id=at(t // 2, z, lax.rem(t, 2), y), device_id_type=MESH)
    for i in range(1, Z):
        pl.semaphore_signal(barrier, inc=1, device_id=at(x, lax.rem(z + i, Z), h, y), device_id_type=MESH)
    for i in range(1, Y):
        for k in range(2):
            pl.semaphore_signal(barrier, inc=1, device_id=at(x, z, k, lax.rem(y + i, Y)), device_id_type=MESH)
    down = lax.broadcasted_iota(jnp.int32, (PAD, PAD), 0)
    across = lax.broadcasted_iota(jnp.int32, (PAD, PAD), 1)
    eye[...] = jnp.where(down == across, 1.0, 0.0).astype(BF16)
    for buf in (rh, ro, eh, eo):
        buf[:, SLOTS:, :] = jnp.zeros((Z, PAD - SLOTS, half), BF16)
    fin[SLOTS:, :] = jnp.zeros((PAD - SLOTS, half), BF16)
    for s in range(mid + 1):
        va[v, s] = jnp.zeros((8, PAD), F32)
        vg[v, s] = jnp.zeros((8, PAD), F32)
    genc_ref[...] = jnp.zeros_like(genc_ref)
    gdec_ref[...] = jnp.zeros_like(gdec_ref)

    for c in small_in:
        c.wait()
    starts = lax.broadcasted_iota(jnp.int32, (rd, TOPK), 1) * STRIDE
    first = lax.broadcasted_iota(jnp.int32, (16, rd), 0) == 0
    picked = jnp.where(first, picks_ref[0:1, :], picks_ref[1:2, :]).astype(F32).astype(BF16)
    small = lax.broadcasted_iota(jnp.int32, (rd, rd), 0) == lax.broadcasted_iota(jnp.int32, (rd, rd), 1)
    pick_columns = nt(jnp.where(small, 1.0, 0.0).astype(BF16), picked)
    meta_ref[...] = jnp.concatenate(
        [(ids_ref[:, k, :] - starts).astype(F32) for k in range(2)]
        + [pick_columns, jnp.zeros((rd, META - 2 * TOPK - 16), F32)],
        axis=1,
    ).astype(BF16)
    xmeta[block(b), :] = meta_ref[...]
    xbuf[block(b), :] = rows_ref[:, lanes(h)]
    pl.semaphore_wait(barrier, nb - 1 + Z - 1 + 2 * (Y - 1))

    def part_lanes(k, q):
        return pl.ds(pl.multiple_of(k * half + q * piece, 128), piece)

    def near(i):
        t = lax.rem(b + i, nb)
        return lax.rem(t, 2), at(t // 2, z, lax.rem(t, 2), y)

    def route_copy(i):
        _, to = near(i)
        return remote(meta_ref, xmeta.at[block(b)], q_send.at[i], q_recv.at[i], to)

    def x_copy(i, q):
        k, to = near(i)
        return remote(
            rows_ref.at[:, part_lanes(k, q)], xbuf.at[block(b), pl.ds(q * piece, piece)],
            x_send.at[i, q], x_recv.at[i, q], to,
        )

    weights = [
        remote(enc_ref.at[lanes(1 - h), :], est.at[h], w_send.at[0], w_recv.at[0], twin),
        remote(dec_ref.at[:, lanes(1 - h)], dech.at[mine], w_send.at[1], w_recv.at[1], twin),
    ]
    for i in range(1, nb):
        route_copy(i).start()
    for q in range(2):
        for i in range(1, nb):
            x_copy(i, q).start()
    for c in weights:
        c.start()

    def turn_encoder(k):
        for i in range(lat // STRIDE):
            low = pl.multiple_of(k * lat + i * STRIDE, STRIDE)
            enct[pl.ds(low, STRIDE), :] = nt(
                eye[...], est[k, :, i * STRIDE : (i + 1) * STRIDE]
            ).astype(BF16)

    for i in range(1, nb):
        route_copy(i).wait_recv()
    nr = xbuf.shape[0]
    meta_t = nt(eye[0:META, 0:META], xmeta[...])
    xf = x.astype(F32)
    hit0 = meta_t[2 * TOPK : 2 * TOPK + 1] == xf
    hit1 = meta_t[2 * TOPK + 1 : 2 * TOPK + 2] == xf
    hit = jnp.where(hit0, 1.0, jnp.where(hit1, 1.0, 0.0))
    offe = jnp.where(hit0, meta_t[0:TOPK], jnp.where(hit1, meta_t[TOPK : 2 * TOPK], 0.0)).astype(BF16)
    before = jnp.where(down[0:nr, 0:nr] < across[0:nr, 0:nr], 1.0, 0.0).astype(BF16)
    rank = nn(jnp.broadcast_to(hit, (16, nr)).astype(BF16), before)[0:1]
    slot = jnp.where(hit > 0.5, rank, -1.0).astype(jnp.int32)
    pm[...] = jnp.where(down[:, 0:nr] == slot, 1.0, 0.0).astype(BF16)

    def ring_copy(buf, send, recv, s, j, q):
        c = chunk_of(s, j)
        view = buf.at[c, pl.ds(0, SLOTS), pl.ds(q * piece, piece)]
        to = at(x, lax.rem(z + (1 - 2 * j) + Z, Z), h, y)
        return remote(view, view, send.at[j, s, q], recv.at[j, s, q], to)

    def ring_wait(buf, send, recv, s, j, q):
        c = chunk_of(s, j)
        view = buf.at[c, pl.ds(0, SLOTS), pl.ds(q * piece, piece)]
        remote(view, view, send.at[j, s - 1, q], recv.at[j, s - 1, q], twin).wait_recv()

    def twin_copy(src, dst, send, recv, s, j):
        c = chunk_of(s, j)
        return remote(src.at[c, pl.ds(0, SLOTS)], dst.at[c, pl.ds(0, SLOTS)], send.at[s, j], recv.at[s, j], twin)

    def order(swap, j, k):
        return 1 - k if swap and j == 1 else k

    def ring_pass(buf, send, recv, s, k, swap):
        for j in range(2):
            q = order(swap, j, k)
            ring_wait(buf, send, recv, s, j, q)
            if q == j:
                ring_copy(buf, send, recv, s, j, q).start()
            else:
                @pl.when(s < mid - 1)
                def _():
                    ring_copy(buf, send, recv, s, j, q).start()

    def ring_begin(buf, send, recv, k, swap):
        for j in range(2):
            ring_copy(buf, send, recv, 0, j, order(swap, j, k)).start()

    def ring_end(buf, send, recv):
        for j in range(2):
            ring_wait(buf, send, recv, mid, j, j)

    def ring_sent(buf, send, recv):
        for s in range(mid):
            for j in range(2):
                for q in range(2):
                    if s < mid - 1 or q == j:
                        ring_copy(buf, send, recv, s, j, q).wait_send()

    def sides(s):
        return (0,) if isinstance(s, int) and s in (0, mid) else (0, 1)

    def run_of(buf, g):
        if buf is va:
            return (pl.ds(0, mid), pl.ds(mid, 1))[g]
        return pl.ds(2 * g, 1 if isinstance(g, int) and 2 * g == mid else 2)

    def value_copy(buf, send, recv, g, i):
        t = lax.rem(v + i, nv)
        view = buf.at[v, run_of(buf, g)]
        return remote(view, view, send.at[g, i], recv.at[g, i], at(x, z, lax.rem(t, 2), t // 2))

    def values_start(buf, send, recv, g):
        for i in range(1, nv):
            value_copy(buf, send, recv, g, i).start()

    def values_wait(buf, send, recv, g):
        for i in range(1, nv):
            view = buf.at[lax.rem(v - i + nv, nv), run_of(buf, g)]
            remote(view, view, send.at[g, i], recv.at[g, i], twin).wait_recv()

    def values_left(buf, send, recv, g):
        for i in range(1, nv):
            value_copy(buf, send, recv, g, i).wait_send()

    def live_at(c, i):
        return lax.broadcasted_iota(jnp.int32, (STRIDE, PAD), 0) == offs[c, pl.ds(i, 1), :].astype(jnp.int32)

    def partial_values(buf, weight, chunks, s):
        for j in sides(s):
            c = chunk_of(s, j)
            dense = nt(weight[...], chunks[c])
            for i in range(BLK):
                buf[v, s, j * BLK + i : j * BLK + i + 1, :] = jnp.sum(
                    jnp.where(live_at(c, i), dense[i * STRIDE : (i + 1) * STRIDE], 0.0), axis=0, keepdims=True
                )

    def whole_values(buf, s):
        total = buf[0, s]
        for k in range(1, nv):
            total += buf[k, s]
        return total

    def spread(values, c, i):
        return jnp.where(live_at(c, i), values, 0.0).astype(BF16)

    def meta_copy(i):
        t = lax.rem(z + i, Z)
        return remote(offs_out.at[t], offs.at[z], m_send.at[i], m_recv.at[i], at(x, t, h, y))

    for q in range(2):
        for i in range(1, nb):
            x_copy(i, q).wait_recv()
        rh[z, :, q * piece : (q + 1) * piece] = nn(pm[...], xbuf[:, q * piece : (q + 1) * piece]).astype(BF16)
        ring_begin(rh, a_send, a_recv, q, False)
        if q == 0:
            offs_t = nt(offe, pm[...])
            for k in range(Z):
                mine = offs_t[k * BLK : (k + 1) * BLK]
                offs_out[k] = jnp.concatenate([mine, mine], axis=0)
            for i in range(1, Z):
                meta_copy(i).start()
            offs[z] = offs_out[z]
    own[0].wait()
    turn_encoder(h)

    def ro_copy():
        return remote(rh.at[:, pl.ds(0, SLOTS)], ro.at[:, pl.ds(0, SLOTS)], d_send.at[0], d_recv.at[0], twin)

    def eo_copy(s, j):
        return twin_copy(eh, eo, f_send, f_recv, s, j)

    def encode(s):
        partial_values(va, enct, rh, s)

    def decode(s):
        values = whole_values(va, s)
        vact[s] = values
        chunks = [chunk_of(s, j) for j in sides(s)]
        table = jnp.concatenate([values] + [offs[c] for c in chunks], axis=0).astype(BF16)
        columns = nt(eye[0:SLOTS, :], table)
        place = lax.broadcasted_iota(jnp.int32, (SLOTS, STRIDE), 1).astype(F32)
        total = None
        for i in range(BLK):
            acts = [
                jnp.where(place == columns[:, 8 + 8 * j + i : 9 + 8 * j + i], columns[:, BLK * j + i : BLK * j + i + 1], 0.0)
                for j in range(len(chunks))
            ]
            act = acts[0] if len(acts) == 1 else jnp.concatenate(acts, axis=0)
            term = nn(act.astype(BF16), dech[i * STRIDE : (i + 1) * STRIDE, :])
            total = term if total is None else total + term
        for j, c in enumerate(chunks):
            part[c] = total[j * SLOTS : (j + 1) * SLOTS]

    for c in weights:
        c.wait_recv()
    turn_encoder(1 - h)
    own[1].wait()
    encode(0)
    def encode_step(s, carry):
        ring_pass(rh, a_send, a_recv, s, 0, False)
        ring_pass(rh, a_send, a_recv, s, 1, False)

        @pl.when(s == 1)
        def _():
            for i in range(1, Z):
                meta_copy(i).wait_recv()

        encode(s)
        return carry

    lax.fori_loop(1, mid, encode_step, 0)
    values_start(va, va_send, va_recv, 0)
    ring_end(rh, a_send, a_recv)
    encode(mid)
    values_start(va, va_send, va_recv, 1)
    ro_copy().start()
    values_wait(va, va_send, va_recv, 0)
    decode(mid - 1)

    def sum_copy(t, j, q):
        view = pl.ds(q * piece, piece)
        to = at(x, lax.rem(z + (1 - 2 * j) + Z, Z), h, y)
        return remote(
            sbuf.at[j, t - 1, :, view], rbuf.at[j, t - 1, :, view], s_send.at[j, t - 1, q], s_recv.at[j, t - 1, q], to
        )

    def transpose_rows(k, src, s):
        for j in sides(s):
            c = chunk_of(s, j)
            for i in range(half // 256):
                rowst[c, pl.ds(pl.multiple_of(k * half + i * 256, 256), 256), :] = nt(
                    eye[...], src[c, :, i * 256 : (i + 1) * 256]
                ).astype(BF16)

    def sum_step(t, k):
        for j in range(2):
            q = order(True, j, k)
            low = q * piece
            c = chunk_of(t, 1 - j)
            total = part[c, :, low : low + piece]
            if t < mid - 1 or (t < mid and q == j):
                sum_copy(t + 1, j, q).wait_recv()
                total += rbuf[j, t, :, low : low + piece].astype(F32)
            sbuf[j, t - 1, :, low : low + piece] = total.astype(BF16)
            sum_copy(t, j, q).start()

    sum_step(mid - 1, 1)
    decode(mid - 2)
    values_wait(va, va_send, va_recv, 1)
    decode(mid)
    sum_step(mid, 0)
    transpose_rows(h, rh, mid)
    sum_step(mid - 1, 0)
    pmt[...] = nt(eye[0:nr, 0:nr], pm[...]).astype(BF16)
    transpose_rows(h, rh, 0)
    for t in range(mid - 2, 0, -1):
        sum_step(t, 1)
        decode(t - 1)
        transpose_rows(h, rh, t)
        sum_step(t, 0)
    transpose_rows(h, rh, mid - 1)
    ro_copy().wait_recv()
    for s in range(mid + 1):
        transpose_rows(1 - h, ro, s)

    def ret_copy(i, q):
        t = lax.rem(b + i, nb)
        return remote(
            xsend.at[block(t), pl.ds(q * piece, piece)], xret.at[x, :, part_lanes(h, q)],
            r_send.at[i, q], r_recv.at[i, q], at(t // 2, z, lax.rem(t, 2), y),
        )

    def ret_wait(i, q):
        t = lax.rem(b - i + nb, nb)
        view = xret.at[t // 2, :, part_lanes(lax.rem(t, 2), q)]
        remote(view, view, r_send.at[i, q], r_recv.at[i, q], twin).wait_recv()

    def err_copy(i, q):
        t = lax.rem(b + i, nb)
        return remote(
            err_ref.at[:, part_lanes(lax.rem(t, 2), q)], xerr.at[block(b), pl.ds(q * piece, piece)],
            e_send.at[i, q], e_recv.at[i, q], at(t // 2, z, lax.rem(t, 2), y),
        )

    for q in range(2):
        own_lanes = slice(q * piece, (q + 1) * piece)
        for j in range(2):
            sum_copy(1, j, q).wait_recv()
        fin[0:SLOTS, own_lanes] = (
            part[z, :, own_lanes] + rbuf[0, 0, :, own_lanes].astype(F32) + rbuf[1, 0, :, own_lanes].astype(F32)
        ).astype(BF16)
        xsend[:, own_lanes] = nn(pmt[...], fin[:, own_lanes]).astype(BF16)
        for i in range(1, nb):
            ret_copy(i, q).start()
        xret[x, :, part_lanes(h, q)] = xsend[block(b), own_lanes]

    for q in range(2):
        for i in range(1, nb):
            ret_wait(i, q)
        for k in range(2):
            cols = slice(k * half + q * piece, k * half + (q + 1) * piece)
            recon = xret[0, :, cols].astype(F32)
            for e in range(1, X):
                recon += xret[e, :, cols].astype(F32)
            err_ref[:, cols] = (recon - rows_ref[:, cols].astype(F32)).astype(BF16)
        for i in range(1, nb):
            err_copy(i, q).start()
        xerr[block(b), q * piece : (q + 1) * piece] = err_ref[:, part_lanes(h, q)]

    for q in range(2):
        for i in range(1, nb):
            err_copy(i, q).wait_recv()
        eh[z, :, q * piece : (q + 1) * piece] = nn(pm[...], xerr[:, q * piece : (q + 1) * piece]).astype(BF16)
        ring_begin(eh, b_send, b_recv, q, False)

    def latent_grads(s):
        for j in sides(s):
            eo_copy(s, j).start()
        partial_values(vg, dech, eh, s)

    def add_dec(s):
        for j in sides(s):
            eo_copy(s, j).wait_recv()
        nblk = lat // STRIDE
        acts = []
        for j in sides(s):
            c = chunk_of(s, j)
            blocks = [spread(vact[s, pl.ds(j * BLK + h * nblk + i, 1), :], c, h * nblk + i) for i in range(nblk)]
            acts.append((c, jnp.concatenate(blocks, axis=0)))
        for k, src in ((h, eh), (1 - h, eo)):
            gdec_ref[:, lanes(k)] += sum(nn(a, src[c]) for c, a in acts)

    def add_enc(s):
        vpre[s] = whole_values(vg, s)
        for i in range(lat // STRIDE):
            blk = h * (lat // STRIDE) + i
            low = i * STRIDE
            pres = [(chunk_of(s, j), spread(vpre[s, pl.ds(j * BLK + blk, 1), :], chunk_of(s, j), blk)) for j in sides(s)]
            for k in range(2):
                cols = slice(k * half, (k + 1) * half)
                genc_ref[cols, low : low + STRIDE] += sum(nt(rowst[c, cols, :], g) for c, g in pres)

    latent_grads(0)

    def gradient_step(s, carry):
        ring_pass(eh, b_send, b_recv, s, 0, False)

        @pl.when(s == 1)
        def _():
            add_dec(0)

        @pl.when(s == 2)
        def _():
            values_wait(vg, vg_send, vg_recv, 0)
            add_enc(0)

        @pl.when(s == 3)
        def _():
            add_enc(1)

        ring_pass(eh, b_send, b_recv, s, 1, False)
        latent_grads(s)

        @pl.when(lax.rem(s, 2) == 1)
        def _():
            values_start(vg, vg_send, vg_recv, s // 2)

        @pl.when(s > 1)
        def _():
            add_dec(s - 1)

        return carry

    lax.fori_loop(1, mid, gradient_step, 0)
    ring_end(eh, b_send, b_recv)
    latent_grads(mid)
    values_start(vg, vg_send, vg_recv, mid // 2)
    add_dec(mid - 1)
    values_wait(vg, vg_send, vg_recv, mid // 2 - 1)
    add_enc(mid - 2)
    add_enc(mid - 1)
    add_dec(mid)
    values_wait(vg, vg_send, vg_recv, mid // 2)
    add_enc(mid)

    for i in range(1, nb):
        route_copy(i).wait_send()
        for q in range(2):
            x_copy(i, q).wait_send()
            ret_copy(i, q).wait_send()
            err_copy(i, q).wait_send()
    for c in weights:
        c.wait_send()
    for i in range(1, Z):
        meta_copy(i).wait_send()
    ring_sent(rh, a_send, a_recv)
    ring_sent(eh, b_send, b_recv)
    for t in range(mid, 0, -1):
        for j in range(2):
            for q in range(2):
                if t < mid or q == j:
                    sum_copy(t, j, q).wait_send()

    for g in range(2):
        values_left(va, va_send, va_recv, g)
    for g in range(mid // 2 + 1):
        values_left(vg, vg_send, vg_recv, g)
    ro_copy().wait_send()

    def eo_left(s):
        for j in sides(s):
            eo_copy(s, j).wait_send()

    def eo_left_step(s, carry):
        eo_left(s)
        return carry

    eo_left(0)
    lax.fori_loop(1, mid, eo_left_step, 0)
    eo_left(mid)


def write_out(*refs):
    srcs, dsts, sems = refs[:3], refs[3:6], refs[6]
    copies = []
    for src, dst, parts in zip(srcs, dsts, (1, 4, 4)):
        n = src.shape[0] // parts
        for k in range(parts):
            rows = pl.ds(k * n, n)
            copies.append(pltpu.make_async_copy(src.at[rows], dst.at[rows], sems.at[len(copies)]))
    for c in copies:
        c.start()
    for c in copies:
        c.wait()


def per_device(experts, topk, cap, rows_in, expert_picks, latent_ids, enc_weight, dec_weight):
    X, Y = experts, lax.axis_size("chan")
    Z = lax.axis_size("expert") // (2 * X)
    rd, width = rows_in.shape
    lat, half, mid = enc_weight.shape[1], width // 2, Z // 2
    nb, nv = 2 * X, 2 * Y
    slots = min(-(-cap * nb // 16) * 16, PAD)
    vmem, hbm = pl.BlockSpec(memory_space=pltpu.VMEM), pl.BlockSpec(memory_space=pltpu.HBM)
    dma = pltpu.SemaphoreType.DMA
    scratch = [
        pltpu.VMEM(rows_in.shape, BF16),
        pltpu.VMEM((2, rd), jnp.int32),
        pltpu.VMEM(latent_ids.shape, jnp.int32),
        pltpu.VMEM((rd, META), BF16),
        pltpu.VMEM((nb * rd, META), BF16),
        pltpu.VMEM((nb * rd, half), BF16),
        pltpu.VMEM((Z, PAD, half), BF16),
        pltpu.VMEM((Z, PAD, half), BF16),
        pltpu.VMEM((Z, PAD, half), BF16),
        pltpu.VMEM((Z, PAD, half), BF16),
        pltpu.VMEM((Z, width, PAD), BF16),
        pltpu.VMEM((2, half, lat), BF16),
        pltpu.VMEM((2 * lat, half), BF16),
        pltpu.VMEM((2 * lat, half), BF16),
        pltpu.VMEM((PAD, PAD), BF16),
        pltpu.VMEM((PAD, nb * rd), BF16),
        pltpu.VMEM((nb * rd, PAD), BF16),
        pltpu.VMEM((Z, 8, PAD), F32),
        pltpu.VMEM((Z, 8, PAD), F32),
        pltpu.VMEM((nv, mid + 1, 8, PAD), F32),
        pltpu.VMEM((nv, mid + 1, 8, PAD), F32),
        pltpu.VMEM((mid + 1, 8, PAD), F32),
        pltpu.VMEM((mid + 1, 8, PAD), F32),
        pltpu.VMEM((Z, slots, half), F32),
        pltpu.VMEM((2, mid, slots, half), BF16),
        pltpu.VMEM((2, mid, slots, half), BF16),
        pltpu.VMEM((PAD, half), BF16),
        pltpu.VMEM((nb * rd, half), BF16),
        pltpu.VMEM((X, rd, width), BF16),
        pltpu.VMEM((nb * rd, half), BF16),
        dma((6,)),
    ]
    pairs = [(nb,), (2,), (nb, 2), (Z,), (2, nv), (mid // 2 + 1, nv), (2, mid, 2), (2, mid, 2), (2, mid, 2)]
    pairs += [(nb, 2), (nb, 2), (1,), (mid + 1, 2)]
    for shape in pairs:
        scratch += [dma(shape), dma(shape)]
    operands = (rows_in, expert_picks.T, latent_ids, enc_weight, dec_weight)
    results = pl.pallas_call(
        functools.partial(step_kernel, X, Y, Z, slots, topk),
        out_shape=(
            pltpu.VMEM(rows_in.shape, BF16),
            pltpu.VMEM(enc_weight.shape, F32),
            pltpu.VMEM(dec_weight.shape, F32),
        ),
        in_specs=[hbm] * 5,
        out_specs=(vmem, vmem, vmem),
        scratch_shapes=scratch,
        compiler_params=pltpu.CompilerParams(
            collective_id=0, has_side_effects=True, vmem_limit_bytes=46 * 2**20
        ),
    )(*(pltpu.with_memory_space_constraint(a, pltpu.HBM) for a in operands))
    return pl.pallas_call(
        write_out,
        out_shape=tuple(jax.ShapeDtypeStruct(r.shape, r.dtype) for r in results),
        in_specs=[vmem] * 3,
        out_specs=(hbm,) * 3,
        scratch_shapes=[dma((9,))],
        compiler_params=pltpu.CompilerParams(vmem_limit_bytes=2 * 2**20),
    )(*(pltpu.with_memory_space_constraint(r, pltpu.VMEM) for r in results))


def solution(mesh, experts=EXPERTS, topk=TOPK, cap=CAP):
    placed = (
        P("expert", "chan"),
        P("expert", None),
        P("expert", None, None),
        P("chan", "expert"),
        P("expert", "chan"),
    )
    return jax.shard_map(
        functools.partial(per_device, experts, topk, cap),
        mesh=mesh,
        in_specs=placed,
        out_specs=(P("expert", "chan"), P("chan", "expert"), P("expert", "chan")),
        check_vma=False,
    )
```
